32 devices in a mesh: ctx: 8 (over y, x, core), fsdp: 4 (over z).
Axes of the slice: x: 2, y: 2, z: 4, core: 2. Of those that a mesh axis runs over, the one named last changes fastest.
Arguments:
- tokens: bfloat16 [4, 1024, 2048], P('fsdp', 'ctx'), may hold values from -6 to 6
- positions: int32 [4, 1024], P('fsdp', 'ctx'), may hold values from 0 to 1021, as said below
- routes: int32 [4, 1024, 4], P('fsdp', 'ctx'), may hold values from 0 to 7, all different within a row; in each aligned block of 128 rows (0 to 127, 128 to 255, ..., all dimensions but the last counted through in order) at most 128 rows name the same one
- cotangent: bfloat16 [4, 1024, 2048], P('fsdp', 'ctx'), may hold values from -6 to 6
- attn_gain: bfloat16 [2048], P(('ctx', 'fsdp')), may hold values from 0.5 to 1.5
- query_weight: bfloat16 [2048, 2048], P(('ctx', 'fsdp')), may hold values from -0.125 to 0.125
- key_weight: bfloat16 [2048, 2048], P(('ctx', 'fsdp')), may hold values from -0.125 to 0.125
- value_weight: bfloat16 [2048, 2048], P(('ctx', 'fsdp')), may hold values from -0.125 to 0.125
- query_bias: bfloat16 [2048], P(('ctx', 'fsdp')), may hold values from -3 to 3
- key_bias: bfloat16 [2048], P(('ctx', 'fsdp')), may hold values from -3 to 3
- value_bias: bfloat16 [2048], P(('ctx', 'fsdp')), may hold values from -3 to 3
- output_weight: bfloat16 [2048, 2048], P(('ctx', 'fsdp')), may hold values from -0.75 to 0.75
- ffn_gain: bfloat16 [2048], P(('ctx', 'fsdp')), may hold values from 0.5 to 1.5
- router_weight: bfloat16 [2048, 8], P(('ctx', 'fsdp')), may hold values from -0.0625 to 0.0625
- expert_gate: bfloat16 [8, 2048, 1408], P('ctx', 'fsdp'), may hold values from -0.125 to 0.125
- expert_up: bfloat16 [8, 2048, 1408], P('ctx', 'fsdp'), may hold values from -0.125 to 0.125
- expert_down: bfloat16 [8, 1408, 2048], P('ctx', 'fsdp'), may hold values from -0.5 to 0.5
- shared_gate: bfloat16 [2048, 5632], P(('ctx', 'fsdp')), may hold values from -0.125 to 0.125
- shared_up: bfloat16 [2048, 5632], P(('ctx', 'fsdp')), may hold values from -0.125 to 0.125
- shared_down: bfloat16 [5632, 2048], P(('ctx', 'fsdp')), may hold values from -0.15625 to 0.15625
- shared_sigmoid: bfloat16 [2048], P(('ctx', 'fsdp')), may hold values from -0.125 to 0.125
Outputs:
- layer_out: bfloat16 [4, 1024, 2048], P('fsdp', 'ctx')
- grad_tokens: float32 [4, 1024, 2048], P('fsdp', 'ctx')
- grad_attn_gain: float32 [2048], P(('ctx', 'fsdp'))
- grad_query_weight: float32 [2048, 2048], P(('ctx', 'fsdp'))
- grad_key_weight: float32 [2048, 2048], P(('ctx', 'fsdp'))
- grad_value_weight: float32 [2048, 2048], P(('ctx', 'fsdp'))
- grad_query_bias: float32 [2048], P(('ctx', 'fsdp'))
- grad_key_bias: float32 [2048], P(('ctx', 'fsdp'))
- grad_value_bias: float32 [2048], P(('ctx', 'fsdp'))
- grad_output_weight: float32 [2048, 2048], P(('ctx', 'fsdp'))
- grad_ffn_gain: float32 [2048], P(('ctx', 'fsdp'))
- grad_router_weight: float32 [2048, 8], P(('ctx', 'fsdp'))
- grad_expert_gate: float32 [8, 2048, 1408], P('ctx', 'fsdp')
- grad_expert_up: float32 [8, 2048, 1408], P('ctx', 'fsdp')
- grad_expert_down: float32 [8, 1408, 2048], P('ctx', 'fsdp')
- grad_shared_gate: float32 [2048, 5632], P(('ctx', 'fsdp'))
- grad_shared_up: float32 [2048, 5632], P(('ctx', 'fsdp'))
- grad_shared_down: float32 [5632, 2048], P(('ctx', 'fsdp'))
- grad_shared_sigmoid: float32 [2048], P(('ctx', 'fsdp'))
The draws below stay inside these ranges and needn't reach their ends.
Inputs may be any that keep to these rules, and one draw needn't show every extreme that they name: Each row of 1024 positions is three documents in a row, counting 0, 1, 2, ... from each document's first token; the first ends within the first 128 places and the last begins within the last 128 places. In some row the first document is one token and the last is one token. `routes`: A token's 4 experts differ. In the rows of one device (128 tokens, aligned) no expert is named more than 128 times, a bound that some block reaches.
All inputs are finite; a program needn't handle non-finite values.
Results may differ from the reference program's by a relative error of at most 0.04.
Values may be sent and summed in bfloat16 or wider, within the bound.
A program may use at most 448 MiB of HBM per device.

```python
import math
import jax
import jax.numpy as jnp
import numpy as np
from jax import lax

D = 2048
HEADS = 16
HEAD = 128
FFE = 1408
FFS = 5632
TOPK = 4
SEQ_DEV = 128
EXPERTS = 8
LEN = 1024
SEQS = 4
CAP = 128


def draw_positions(key, part):
    key = jax.random.fold_in(key, 11)
    first_key, last_key, row_key = jax.random.split(key, 3)
    first_end = jax.random.randint(first_key, (SEQS,), 1, SEQ_DEV)
    last_start = jax.random.randint(last_key, (SEQS,), LEN - SEQ_DEV + 1, LEN)
    chosen_row = jax.random.randint(row_key, (), 0, SEQS)
    row_ids = jnp.arange(SEQS, dtype=jnp.int32)
    first_end = jnp.where(row_ids == chosen_row, 1, first_end)
    last_start = jnp.where(row_ids == chosen_row, LEN - 1, last_start)
    places = jnp.arange(LEN, dtype=jnp.int32)[None, :]
    starts = jnp.where(places >= last_start[:, None], last_start[:, None], jnp.where(places >= first_end[:, None], first_end[:, None], 0))
    return (places - starts).astype(jnp.int32)


def block_levels(own_key, extent, cuts, least, largest):
    def one(dim, blocks):
        draws = jax.random.uniform(jax.random.fold_in(jax.random.fold_in(own_key, 6), dim), (blocks,), jnp.float32, least / len(cuts), largest / len(cuts))
        return jnp.repeat(jnp.exp(draws), extent[dim] // blocks).reshape((-1,) + (1,) * (len(extent) - dim - 1))

    gain = one(*cuts[0])
    for cut in cuts[1:]:
        gain = gain * one(*cut)
    return gain


def routed_block(rng, own, number, rows, amount, top, bound, slope):
    order = jax.random.permutation(rng, amount)
    crowded, common = load_shares(amount, rows * top, bound, slope, True), load_shares(amount, rows * top, bound, slope, False)
    places = jnp.arange(amount)

    def named(lengths, turn):
        used = int((lengths > 0).sum())
        fixed = max(1, used // 4)
        moved = fixed + (places - fixed + turn * (used - fixed)) % max(1, amount - fixed)
        return jnp.zeros((amount,), jnp.int32).at[order[jnp.where(places < fixed, places, moved)]].set(jnp.asarray(lengths, jnp.int32))

    lengths = jnp.where(number % 4 == 0, named(crowded, number // 4), named(common, number - number // 4 - 1))
    mixed = jax.random.permutation(jax.random.fold_in(own, 3), amount)
    giver, sink = mixed[0:amount // 2 * 2:2], mixed[1:amount // 2 * 2:2]
    room = jnp.minimum(lengths[giver] - 1, bound - lengths[sink]) // 2
    room = jnp.where((giver == order[0]) | (sink == order[0]) | (lengths[sink] == 0), 0, jnp.maximum(room, 0))
    moved = jax.random.randint(jax.random.fold_in(own, 4), (amount // 2,), 0, 1 << 20) % (room + 1)
    lengths = lengths.at[giver].add(-moved).at[sink].add(moved)
    members = jnp.searchsorted(jnp.cumsum(lengths), jnp.arange(rows * top), side="right").astype(jnp.int32)
    table = members.reshape(top, rows).T
    table = table[jax.random.permutation(jax.random.fold_in(own, 1), rows)]
    turn = jax.random.randint(jax.random.fold_in(own, 2), (rows, 1), 0, top)
    return jnp.take_along_axis(table, (jnp.arange(top)[None, :] + turn) % top, axis=1)


def load_shares(count, total, most, skew, full):
    weights = [(1 << 20) // math.isqrt(rank ** skew) + 1 for rank in range(1, count + 1)]
    largest = most if full else min(most, max(-(-total // count), total * weights[0] // sum(weights)))
    least = 1 if total - largest >= count - 1 else 0
    given, spare = [largest] + [least] * (count - 1), total - largest - least * (count - 1)
    while spare > 0:
        free = [i for i in range(1, count) if given[i] < largest] or [i for i in range(1, count) if given[i] < most]
        pool, left = sum([weights[i] for i in free]), spare
        for i in free:
            more = min(most - given[i], max(1, left * weights[i] // pool), spare)
            given[i] = given[i] + more
            spare = spare - more
    return np.array(given)


def bell_draw(stream_key, dims, scale, reach, cuts=(), kind=jnp.bfloat16):
    array = scale * jax.random.normal(stream_key, dims, jnp.float32)
    if cuts:
        array = array * block_levels(stream_key, dims, cuts, -0.22, 0.18)
    return jnp.clip(array, -reach, reach).astype(kind)


def setup_inputs(seed: int = 0) -> dict:
    streams_of = jax.random.split(jax.random.key(seed), 22)
    tokens = bell_draw(streams_of[0], (SEQS, LEN, D), 1.0, 6.0, ((0, 4), (1, 8)))
    positions = draw_positions(jax.random.fold_in(streams_of[21], 71), 0)
    routes_keys = jax.random.split(jax.random.fold_in(streams_of[2], 1), SEQS * LEN // SEQ_DEV)
    routes_turns = jax.random.permutation(jax.random.fold_in(streams_of[2], 3), SEQS * LEN // SEQ_DEV)
    routes = jax.vmap(lambda own, number: routed_block(jax.random.fold_in(streams_of[2], 2), own, number, SEQ_DEV, EXPERTS, TOPK, CAP, 1))(routes_keys, routes_turns).reshape((SEQS, LEN, TOPK))
    cotangent = bell_draw(streams_of[3], (SEQS, LEN, D), 1.0, 6.0, ((0, 4), (1, 8)))
    attn_gain = jnp.clip(1.0 + 0.1 * jax.random.normal(streams_of[4], (D,), jnp.float32), 0.5, 1.5).astype(jnp.bfloat16)
    query_weight = bell_draw(streams_of[5], (D, D), D ** -0.5, 0.125, ((0, 32),))
    key_weight = bell_draw(streams_of[6], (D, D), D ** -0.5, 0.125, ((0, 32),))
    value_weight = bell_draw(streams_of[7], (D, D), D ** -0.5, 0.125, ((0, 32),))
    query_bias = bell_draw(streams_of[8], (D,), 0.3, 3.0, ((0, 32),))
    key_bias = bell_draw(streams_of[9], (D,), 0.3, 3.0, ((0, 32),))
    value_bias = bell_draw(streams_of[10], (D,), 0.3, 3.0, ((0, 32),))
    output_weight = bell_draw(streams_of[11], (D, D), (D // 32) ** -0.5, 0.75, ((0, 32),))
    ffn_gain = jnp.clip(1.0 + 0.1 * jax.random.normal(streams_of[12], (D,), jnp.float32), 0.5, 1.5).astype(jnp.bfloat16)
    router_weight = bell_draw(streams_of[13], (D, EXPERTS), (4 * D) ** -0.5, 0.0625, ((0, 32),))
    expert_gate = bell_draw(streams_of[14], (EXPERTS, D, FFE), D ** -0.5, 0.125, ((0, 8), (1, 4)))
    expert_up = bell_draw(streams_of[15], (EXPERTS, D, FFE), D ** -0.5, 0.125, ((0, 8), (1, 4)))
    expert_down = bell_draw(streams_of[16], (EXPERTS, FFE, D), (max(1, FFE * 6 // (EXPERTS * EXPERTS))) ** -0.5, 0.5, ((0, 8), (1, 4)))
    shared_gate = bell_draw(streams_of[17], (D, FFS), D ** -0.5, 0.125, ((0, 32),))
    shared_up = bell_draw(streams_of[18], (D, FFS), D ** -0.5, 0.125, ((0, 32),))
    shared_down = bell_draw(streams_of[19], (FFS, D), (FFS // 4) ** -0.5, 0.15625, ((0, 32),))
    shared_sigmoid = bell_draw(streams_of[20], (D,), D ** -0.5, 0.125, ((0, 32),))
    return {"tokens": tokens, "positions": positions, "routes": routes, "cotangent": cotangent, "attn_gain": attn_gain, "query_weight": query_weight, "key_weight": key_weight, "value_weight": value_weight, "query_bias": query_bias, "key_bias": key_bias, "value_bias": value_bias, "output_weight": output_weight, "ffn_gain": ffn_gain, "router_weight": router_weight, "expert_gate": expert_gate, "expert_up": expert_up, "expert_down": expert_down, "shared_gate": shared_gate, "shared_up": shared_up, "shared_down": shared_down, "shared_sigmoid": shared_sigmoid}


EPS = 1e-06
ROPE_BASE = 1000000.0
MASKED = -1e+30

@jax.custom_vjp
def low(v):
    return lax.optimization_barrier(v.astype(jnp.bfloat16)).astype(jnp.float32)

@jax.custom_vjp
def low_back(v):
    return v

def low_keep(v):
    return (low(v), None)

def low_pass(kept, grad):
    return (grad,)

def back_keep(v):
    return (v, None)

def back_low(kept, grad):
    return (low(grad),)
low.defvjp(low_keep, low_pass)
low_back.defvjp(back_keep, back_low)

def product(left, right):
    return jnp.dot(left, right, precision=lax.Precision.HIGHEST)

def rms_scale(values):
    return lax.rsqrt(lax.optimization_barrier(jnp.mean(values * values, axis=-1, keepdims=True)) + EPS)

def rope_tables(places, head_size):
    half = head_size // 2
    freqs = jnp.exp(jnp.arange(half, dtype=jnp.float32) * (-2.0 * math.log(ROPE_BASE) / head_size))
    angles = places.astype(jnp.float32)[:, None] * freqs[None, :]
    return (jnp.cos(angles), jnp.sin(angles))

def rotate(values, cosine, sine):
    half = values.shape[-1] // 2
    first = values[..., :half]
    second = values[..., half:]
    cosine = cosine[:, None, :]
    sine = sine[:, None, :]
    return jnp.concatenate([first * cosine - second * sine, second * cosine + first * sine], axis=-1)

def attention(queries, keys, values, places):
    length = queries.shape[0]
    block = math.gcd(length, 512)
    glob = jnp.arange(length, dtype=jnp.int32)
    starts = glob - places.astype(jnp.int32)
    scale = 1.0 / math.sqrt(HEAD)

    def one_block(index):
        lower = (index * block).astype(jnp.int32)
        rows = lax.dynamic_slice_in_dim(queries, lower, block, 0)
        row_glob = lax.dynamic_slice_in_dim(glob, lower, block, 0)
        row_start = lax.dynamic_slice_in_dim(starts, lower, block, 0)
        scores = low_back(jnp.einsum('qhd,khd->hqk', rows, keys, precision=lax.Precision.HIGHEST) * scale)
        mask = (glob[None, :] <= row_glob[:, None]) & (glob[None, :] >= row_start[:, None])
        scores = jnp.where(mask[None], scores, MASKED)
        weights = jax.nn.softmax(scores, axis=-1)
        return jnp.einsum('hqk,khd->qhd', low(weights), values, precision=lax.Precision.HIGHEST)
    blocks = lax.map(jax.checkpoint(one_block), jnp.arange(length // block, dtype=jnp.int32))
    return blocks.reshape(length, HEADS, HEAD)

def layer(states, places, chosen, weights):
    attn_gain, w_query, w_key, w_value, b_query, b_key, b_value, w_output, ffn_gain, w_router, expert_gate, expert_up, expert_down, shared_gate, shared_up, shared_down, shared_sigmoid = weights
    length = states.shape[0]
    normed = low(states * rms_scale(states) * attn_gain)
    cosine, sine = rope_tables(places, HEAD)
    query_pre = low_back(product(normed, w_query) + b_query)
    key_pre = low_back(product(normed, w_key) + b_key)
    values = low(low_back(product(normed, w_value) + b_value)).reshape(length, HEADS, HEAD)
    queries = low(rotate(query_pre.reshape(length, HEADS, HEAD), cosine, sine))
    keys = low(rotate(key_pre.reshape(length, HEADS, HEAD), cosine, sine))
    mixed = attention(queries, keys, values, places)
    attn_low = low(low_back(mixed)).reshape(length, HEADS * HEAD)
    mid = states + low_back(product(attn_low, w_output))
    normed2 = low(mid * rms_scale(mid) * ffn_gain)
    logits = low_back(product(normed2, w_router))
    router_probs = jax.nn.softmax(logits, axis=-1)
    expert_ids = jnp.arange(w_router.shape[1], dtype=jnp.int32)
    hits = lax.optimization_barrier(jnp.sum((chosen.astype(jnp.int32)[:, :, None] == expert_ids[None, None, :]).astype(jnp.float32), axis=1))
    table = (router_probs * hits).T

    def expert_term(carry, items):
        w_gate, w_up, w_down, column = items
        routed = low_back(normed2)
        gate_pre = low_back(product(routed, w_gate))
        up_pre = low_back(product(routed, w_up))
        hidden = low(jax.nn.silu(gate_pre) * up_pre)
        result = low(low_back(product(hidden, w_down)))
        return (carry + column[:, None] * result, None)
    mixture, unused = lax.scan(jax.checkpoint(expert_term), jnp.zeros_like(states), (expert_gate, expert_up, expert_down, table))
    shared_gate_pre = low_back(product(normed2, shared_gate))
    shared_up_pre = low_back(product(normed2, shared_up))
    shared_hidden = low(jax.nn.silu(shared_gate_pre) * shared_up_pre)
    shared_out = low_back(product(shared_hidden, shared_down))
    switch = jax.nn.sigmoid(product(normed2, shared_sigmoid))
    return mid + mixture + switch[:, None] * shared_out

def reference(tokens, positions, routes, cotangent, attn_gain, query_weight, key_weight, value_weight, query_bias, key_bias, value_bias, output_weight, ffn_gain, router_weight, expert_gate, expert_up, expert_down, shared_gate, shared_up, shared_down, shared_sigmoid):
    weights = tuple((w.astype(jnp.float32) for w in (attn_gain, query_weight, key_weight, value_weight, query_bias, key_bias, value_bias, output_weight, ffn_gain, router_weight, expert_gate, expert_up, expert_down, shared_gate, shared_up, shared_down, shared_sigmoid)))
    inputs = tokens.astype(jnp.float32)

    def forward(inputs, weights):

        def one_sequence(carry, items):
            states, places, chosen = items
            return (carry, layer(states, places, chosen, weights))
        unused, outputs = lax.scan(one_sequence, jnp.zeros((), jnp.float32), (inputs, positions, routes))
        return outputs
    outputs, pullback = jax.vjp(forward, inputs, weights)
    grad_inputs, grads = pullback(cotangent.astype(jnp.float32))
    return (outputs.astype(jnp.bfloat16), grad_inputs, grads[0], grads[1], grads[2], grads[3], grads[4], grads[5], grads[6], grads[7], grads[8], grads[9], grads[10], grads[11], grads[12], grads[13], grads[14], grads[15], grads[16])
```

```python
import functools
import math

import jax
import jax.numpy as jnp
from jax import lax
from jax.experimental import pallas as pl
from jax.experimental.pallas import tpu as pltpu
from jax.sharding import PartitionSpec as P

HEADS = 16
HEAD = 128
EPS = 1e-06
ROPE_BASE = 1000000.0
MASKED = -1e30
BLOCK = 1024
BOTH = ("ctx", "fsdp")
BF16 = jnp.bfloat16
F32 = jnp.float32


PLANE, LINE = 8, 4
LANES = 128
HBM = pl.BlockSpec(memory_space=pl.ANY)
VMEM = pl.BlockSpec(memory_space=pltpu.VMEM)


class Place:
    def __init__(self):
        self.c = lax.axis_index("ctx")
        self.z = lax.axis_index("fsdp")
        self.core = self.c % 2
        self.x = (self.c // 2) % 2
        self.y = self.c // 4
        self.twin = self.c + 1 - 2 * self.core
        self.across = self.c + 2 - 4 * self.x
        self.along = self.c + 4 - 8 * self.y
        self.far = self.across + 4 - 8 * self.y
        self.upper = self.z // 2
        self.depth = self.z + self.upper * (3 - 2 * self.z)
        self.near = self.z + 1 - 2 * (self.z % 2)
        self.middle = 3 - self.z

    def mirrored(self, number):
        return number + self.upper * (3 - 2 * number)

    def plane(self, c):
        return (c, self.z)

    def line(self, z):
        return (self.c, z)

    def on_line(self):
        return [(self.z + step) % LINE for step in (2, 1, 3)]


class Wire:
    def __init__(self, send, recv):
        self.send, self.recv, self.used, self.open = send, recv, 0, []

    def copy(self, source, target, device, arrival=None):
        number = self.used
        self.used += 1
        return pltpu.make_async_remote_copy(
            src_ref=source,
            dst_ref=target,
            send_sem=self.send.at[number],
            recv_sem=self.recv.at[number if arrival is None else arrival],
            device_id=device,
            device_id_type=pl.DeviceIdType.MESH,
        )

    def later(self, source, target, device, arrival=None):
        copy = self.copy(source, target, device, arrival)
        self.open.append(copy)
        return copy

    def push(self, source, target, device):
        copy = self.later(source, target, device)
        copy.start()
        return copy

    def close(self):
        for copy in self.open:
            copy.wait_send()


def greet(devices):
    barrier = pltpu.get_barrier_semaphore()
    for device in devices:
        pl.semaphore_signal(
            barrier, inc=1, device_id=device, device_id_type=pl.DeviceIdType.MESH
        )
    pl.semaphore_wait(barrier, len(devices))


class PlaneGather:
    def __init__(self, wire, here, at, source=None):
        source = at(here.c) if source is None else source
        to_x, to_y = here.plane(here.across), here.plane(here.along)
        to_twin = here.plane(here.twin)
        x_block, y_block, far_block = at(here.across), at(here.along), at(here.far)
        half = x_block.shape[0] // 2
        high, low = x_block.at[pl.ds(half, half)], y_block.at[pl.ds(0, half)]
        self.from_x = wire.later(source, at(here.c), to_x)
        self.from_y = wire.later(source, at(here.c), to_y)
        self.far_y = wire.later(high, high, to_y)
        self.far_x = wire.later(low, low, to_x)
        blocks = [(source, at(here.c))] + [(b, b) for b in (x_block, y_block, far_block)]
        self.twins = [wire.later(block, target, to_twin) for block, target in blocks]

    def first(self):
        self.from_x.start()
        self.from_y.start()
        self.twins[0].start()
        return self

    def second(self):
        self.from_x.wait_recv()
        self.far_y.start()
        self.twins[1].start()
        self.from_y.wait_recv()
        self.far_x.start()
        self.twins[2].start()

    def third(self):
        self.far_x.wait_recv()
        self.far_y.wait_recv()
        self.twins[3].start()

    def finish(self):
        for copy in self.twins:
            copy.wait_recv()


PLANE_GATHER_COPIES = 8


class LineGather:
    def __init__(self, wire, here, at, source=None):
        self.wire, self.here, self.at = wire, here, at
        source = at(here.z) if source is None else source
        self.one = wire.push(source, at(here.z), here.line(here.near))
        inner = here.depth == 1
        middle, near = here.line(here.middle), here.line(here.near)
        own, mine = source, at(here.z)
        end, two, three = at(here.mirrored(0)), at(here.mirrored(2)), at(here.mirrored(3))
        self.inner = inner
        self.two_in = wire.copy(own, mine, middle)
        self.three_in = wire.copy(end, end, middle)
        self.two_out = wire.copy(two, two, near)
        self.three_out = wire.copy(three, three, near)

        @pl.when(inner)
        def _():
            self.two_in.start()

    def first(self):
        self.one.wait_recv()
        pl.when(self.inner)(self.three_in.start)

    def second(self):
        @pl.when(self.inner)
        def _():
            self.two_in.wait_recv()
            self.two_out.start()

        @pl.when(self.here.depth == 0)
        def _():
            self.two_out.wait_recv()

    def third(self):
        @pl.when(self.inner)
        def _():
            self.three_in.wait_recv()
            self.three_out.start()

        @pl.when(self.here.depth == 0)
        def _():
            self.three_out.wait_recv()

    def order(self):
        here = self.here
        return [here.z, here.near, here.mirrored(2), here.mirrored(3)]

    def finish(self):
        @pl.when(self.inner)
        def _():
            for copy in (self.two_in, self.three_in, self.two_out, self.three_out):
                copy.wait_send()


LINE_GATHER_COPIES = 5


def add_into(total, part):
    rows = total.shape[0]
    step = min(rows, 32)

    @pl.loop(0, rows // step)
    def _(i):
        at = pl.ds(pl.multiple_of(i * step, step), step)
        total[at] = total[at] + part[at]


class PlaneScatter:
    def __init__(self, wire, here, parts, room):
        self.here, self.parts, self.room = here, parts, room
        arrived, one_x, one_y, two_x, two_y = room
        self.half = arrived.shape[1] // 2
        to_x, to_y = here.plane(here.across), here.plane(here.along)
        self.twin = wire.later(parts.at[:, 1 - here.core], arrived, here.plane(here.twin))
        self.from_x = [
            wire.later(self.block(y, 1 - here.x, 0), one_x.at[y], to_x) for y in range(2)
        ]
        self.from_y = [
            wire.later(self.block(1 - here.y, x, 1), one_y.at[x], to_y) for x in range(2)
        ]
        self.last_y = wire.later(self.block(1 - here.y, here.x, 0), two_y, to_y)
        self.last_x = wire.later(self.block(here.y, 1 - here.x, 1), two_x, to_x)

    def block(self, y, x, half=None):
        if half is None:
            return self.parts.at[y * 2 + x, self.here.core]
        return self.parts.at[y * 2 + x, self.here.core, pl.ds(half * self.half, self.half)]

    def begin(self):
        self.twin.start()

    def first(self):
        self.twin.wait_recv()
        for i in range(4):
            add_into(self.parts.at[i, self.here.core], self.room[0].at[i])
        for copy in self.from_x + self.from_y:
            copy.start()

    def second(self):
        here, one_x, one_y = self.here, self.room[1], self.room[2]
        for copy in self.from_x:
            copy.wait_recv()
        add_into(self.block(1 - here.y, here.x, 0), one_x.at[1 - here.y])
        self.last_y.start()
        for copy in self.from_y:
            copy.wait_recv()
        add_into(self.block(here.y, 1 - here.x, 1), one_y.at[1 - here.x])
        self.last_x.start()
        add_into(self.block(here.y, here.x, 0), one_x.at[here.y])
        add_into(self.block(here.y, here.x, 1), one_y.at[here.x])

    def third(self):
        here, two_x, two_y = self.here, self.room[3], self.room[4]
        self.last_y.wait_recv()
        add_into(self.block(here.y, here.x, 0), two_y)
        self.last_x.wait_recv()
        add_into(self.block(here.y, here.x, 1), two_x)

    def mine(self):
        return self.block(self.here.y, self.here.x)


PLANE_SCATTER_COPIES = 7


class LineScatter:
    def __init__(self, wire, here, blocks, room):
        self.here, self.blocks = here, blocks
        near, middle = here.line(here.near), here.line(here.middle)
        self.ends, self.mids = room
        own = self.blocks
        self.out = [wire.copy(own[i], self.ends.at[k], near) for k, i in enumerate((2, 3, 1))]
        self.over = [wire.copy(own[i], self.mids.at[k], middle) for k, i in enumerate((2, 3))]
        self.home = wire.copy(own[0], self.ends.at[0], near)

    def begin(self):
        @pl.when(self.here.depth == 0)
        def _():
            for copy in self.out:
                copy.start()

    def first(self):
        @pl.when(self.here.depth == 1)
        def _():
            for k in range(2):
                self.out[k].wait_recv()
                add_into(self.blocks[2 + k], self.ends.at[k])
                self.over[k].start()

    def second(self):
        @pl.when(self.here.depth == 1)
        def _():
            self.over[1].wait_recv()
            add_into(self.blocks[0], self.mids.at[1])
            self.home.start()
            self.out[2].wait_recv()
            add_into(self.blocks[1], self.ends.at[2])
            self.over[0].wait_recv()
            add_into(self.blocks[1], self.mids.at[0])

    def third(self):
        @pl.when(self.here.depth == 0)
        def _():
            self.home.wait_recv()
            add_into(self.blocks[0], self.ends.at[0])
            for copy in self.out:
                copy.wait_send()

        @pl.when(self.here.depth == 1)
        def _():
            for copy in self.over + [self.home]:
                copy.wait_send()


LINE_SCATTER_COPIES = 6


def scatter_room(rows, columns, kind):
    half = rows // 2
    return [
        pltpu.VMEM((4, rows, columns), kind),
        pltpu.VMEM((2, half, columns), kind),
        pltpu.VMEM((2, half, columns), kind),
        pltpu.VMEM((half, columns), kind),
        pltpu.VMEM((half, columns), kind),
    ]


def wires(count):
    return [pltpu.SemaphoreType.DMA((count,)), pltpu.SemaphoreType.DMA((count,))]


def call(kernel, number, outs, args, scratch, out_specs=None, in_specs=None, aliases=None):
    return pl.pallas_call(
        kernel,
        out_shape=[jax.ShapeDtypeStruct(shape, kind) for shape, kind in outs],
        in_specs=in_specs or [HBM] * len(args),
        out_specs=out_specs or [HBM] * len(outs),
        scratch_shapes=scratch,
        input_output_aliases=aliases or {},
        compiler_params=pltpu.CompilerParams(
            collective_id=number, has_side_effects=True, vmem_limit_bytes=60 << 20
        ),
    )(*args)


def start_kernel(
    tokens, three, output, small, shared, later, x_out, three_out, output_out, small_out,
    shared_out, later_out, send, recv, local
):
    here, wire = Place(), Wire(send, recv)
    others = [(here.c + step) % PLANE for step in range(1, PLANE)]
    greet([here.plane(c) for c in others] + [here.line(z) for z in here.on_line()])
    small_line = [
        wire.push(small, small_out.at[here.c, here.z], here.line(z)) for z in here.on_line()
    ]
    plane = [
        wire.push(three.at[c], three_out.at[here.c, here.z], here.plane(c)) for c in others
    ]
    mine = [
        pltpu.make_async_copy(small, small_out.at[here.c, here.z], local.at[0]),
        pltpu.make_async_copy(three.at[here.c], three_out.at[here.c, here.z], local.at[1]),
        pltpu.make_async_copy(tokens, x_out.at[here.c], local.at[2]),
        pltpu.make_async_copy(output, output_out.at[here.z], local.at[3]),
        pltpu.make_async_copy(shared.at[here.c], shared_out.at[:, here.c], local.at[4]),
    ]
    for copy in mine:
        copy.start()
    x_plane = PlaneGather(wire, here, lambda c: x_out.at[c], tokens).first()
    for copy in mine:
        copy.wait()
    for copy in small_line + plane:
        copy.wait_recv()
    three_line = LineGather(wire, here, lambda z: three_out.at[:, z])
    output_line = LineGather(wire, here, lambda z: output_out.at[z])
    small_plane = PlaneGather(wire, here, lambda c: small_out.at[c]).first()
    swapped = [
        wire.push(shared.at[c], shared_out.at[:, here.c], here.plane(c)) for c in others
    ]
    x_plane.second()
    small_plane.second()
    x_plane.third()
    small_plane.third()
    three_line.first()
    output_line.first()
    three_line.second()
    output_line.second()
    three_line.third()
    output_line.third()
    x_plane.finish()
    small_plane.finish()
    for copy in swapped:
        copy.wait_recv()
    three_line.finish()
    output_line.finish()
    wire.close()


def start_transfers(tokens, three, output, small, shared, later):
    rows, width = tokens.shape
    _, owned, wide = three.shape
    copies = 3 + 7 + 7 + 2 * PLANE_GATHER_COPIES + 2 * LINE_GATHER_COPIES
    return call(
        start_kernel,
        1,
        [
            ((PLANE, rows, width), BF16),
            ((PLANE, LINE, owned, wide), BF16),
            ((LINE, owned, width), BF16),
            ((PLANE, LINE) + small.shape, BF16),
            ((LINE, PLANE) + shared.shape[2:], BF16),
            (later.shape, later.dtype),
        ],
        [tokens, three, output, small, shared, later],
        wires(copies) + [pltpu.SemaphoreType.DMA((5,))],
        in_specs=[VMEM] * 5 + [HBM],
        aliases={5: 5},
    )


def fold_kernel(parts, shared, out, shared_out, *scratch):
    here, wire = Place(), Wire(scratch[0], scratch[1])
    local = scratch[2]
    greet(
        [here.plane(c) for c in (here.twin, here.across, here.along)]
        + [here.line(z) for z in here.on_line()]
    )
    kept = pltpu.make_async_copy(shared.at[here.z], shared_out.at[:, here.z], local.at[2])
    kept.start()
    moved = [
        wire.push(shared.at[z], shared_out.at[:, here.z], here.line(z)) for z in here.on_line()
    ]
    half = parts.shape[2] // 2
    jobs, loads = [], []
    for i in range(2):
        held, room = scratch[3 + 6 * i], scratch[4 + 6 * i : 9 + 6 * i]
        loads.append(
            pltpu.make_async_copy(parts.at[:, :, pl.ds(i * half, half)], held, local.at[i])
        )
        loads[i].start()
        jobs.append(PlaneScatter(wire, here, held, room))
    for load, job in zip(loads, jobs):
        load.wait()
        job.begin()
    for job in jobs:
        job.first()
    for job in jobs:
        job.second()
    for i, job in enumerate(jobs):
        job.third()
        out[pl.ds(i * half, half)] = job.mine()[...].astype(out.dtype)
    for copy in moved:
        copy.wait_recv()
    kept.wait()
    wire.close()


def held_room(rows, columns, kind):
    return [pltpu.VMEM((4, 2, rows, columns), kind)] + scatter_room(rows, columns, kind)


def fold_plane(parts, shared):
    rows, width = parts.shape[0] // PLANE, parts.shape[1]
    return call(
        fold_kernel,
        3,
        [((rows, width), F32), ((PLANE, LINE) + shared.shape[2:], BF16)],
        [parts.reshape(4, 2, rows, width), shared],
        wires(2 * PLANE_SCATTER_COPIES + 3)
        + [pltpu.SemaphoreType.DMA((3,))]
        + held_room(rows // 2, width, BF16) * 2,
        out_specs=[VMEM, HBM],
    )


STEPS, TILE = 8, 512


def ffn_kernel(
    x, few, g, mixed, shared, routed_down, shared_down, x_out, sum_out, dots_out, out_parts, pre_out, weighted_out,
    send, recv, local, fetch, store, w_both, w_down, few_all, parts, landed, dots_parts, dots_landed,
    x_buf, g_buf, o_buf, p_buf, h_buf, pre_buf, back_buf, by_buf, dot_buf, *rooms
):
    here, wire = Place(), Wire(send, recv)
    rows, width = x.shape
    chunk = 4 * rows
    routed, units = routed_down.shape[0], w_down.shape[0]
    used = routed + shared_down.shape[0]
    few_rows = few.shape[0]
    greet(
        [here.plane(c) for c in (here.twin, here.across, here.along)]
        + [here.line(z) for z in here.on_line()]
    )
    own = pltpu.make_async_copy(x, x_out.at[here.z, here.c], local.at[0])
    own.start()
    own_few = pltpu.make_async_copy(few, few_all.at[here.c, here.z], local.at[1])
    own_few.start()
    part = mixed.shape[2]
    pieces = [
        (mixed.at[z, pl.ds(k * routed, routed)], w_both.at[pl.ds(k * units, routed), pl.ds(z * part, part)])
        for z in range(LINE)
        for k in range(2)
    ]
    pieces += [
        (
            shared.at[pl.ds(k * (used - routed), used - routed)],
            w_both.at[pl.ds(k * units + routed, used - routed)],
        )
        for k in range(2)
    ]
    pieces += [
        (routed_down, w_down.at[pl.ds(0, routed)]),
        (shared_down, w_down.at[pl.ds(routed, used - routed)]),
    ]
    weights = [
        pltpu.make_async_copy(source, target, local.at[2 + i])
        for i, (source, target) in enumerate(pieces)
    ]
    for copy in weights:
        copy.start()
    nothing = jnp.zeros((units - used, width), BF16)
    w_both[pl.ds(used, units - used)] = nothing
    w_both[pl.ds(units + used, units - used)] = nothing
    w_down[pl.ds(used, units - used)] = nothing
    few_line = [
        wire.push(few, few_all.at[here.c, here.z], here.line(z)) for z in here.on_line()
    ]
    line = LineGather(wire, here, lambda z: x_out.at[z, here.c], x)
    order = line.order()
    planes = [
        PlaneGather(
            wire, here, functools.partial(lambda z, c: x_out.at[z, c], order[i]), None if i else x
        )
        for i in range(4)
    ]
    few_plane = PlaneGather(wire, here, lambda c: few_all.at[c])
    jobs = [PlaneScatter(wire, here, parts.at[i], rooms[5 * i : 5 * i + 5]) for i in range(4)]
    dots_jobs = [
        PlaneScatter(wire, here, dots_parts.at[i], rooms[20 + 5 * i : 25 + 5 * i])
        for i in range(4)
    ]
    slots = [None, 0, 1 + here.depth, 2 - here.depth]
    base = wire.used
    arrivals = [
        wire.copy(source.at[0, 0, 0], target.at[slot], here.line(here.near))
        for source, target in ((parts, landed), (dots_parts, dots_landed))
        for slot in range(3)
    ]
    lines = [
        wire.later(job.mine(), target.at[slots[i]], here.line(order[i]), base + 3 * k + slots[i])
        for k, (group, target) in enumerate(((jobs, landed), (dots_jobs, dots_landed)))
        for i, job in enumerate(group)
        if i
    ]
    planes[0].first()
    own.wait()
    own_few.wait()
    for copy in few_line:
        copy.wait_recv()
    few_plane.first()

    def where(step):
        group, half = step // 2, step % 2
        late = group // 2
        number = (here.depth + group) % 2 * (1 - late) + group * late
        return group, here.mirrored(number), (here.y + half) % 2

    def loads(step):
        _, z, y = where(step)
        at = pl.ds(4 * y, 4)
        return [
            pltpu.make_async_copy(x_out.at[z, at], x_buf, fetch.at[0]),
            pltpu.make_async_copy(g.at[z, at], g_buf, fetch.at[1]),
        ]

    def stores(step):
        _, z, y = where(step)
        at = pl.ds(4 * y, 4)
        return [
            pltpu.make_async_copy(o_buf, out_parts.at[z, pl.ds(2 * y, 2)], store.at[0]),
            pltpu.make_async_copy(p_buf, pre_out.at[z, at], store.at[1]),
            pltpu.make_async_copy(h_buf, weighted_out.at[z, at], store.at[2]),
        ]

    def scatter(i, phase):
        for job in (jobs[i], dots_jobs[i]):
            getattr(job, phase)()
        if phase == "third" and i:
            lines[i - 1].start()
            lines[3 + i - 1].start()

    def arrived(step):
        for chip in (0, 1):
            planes[step // 2].twins[step % 2 * 2 + chip].wait_recv()

    def begin(i):
        return functools.partial(scatter, i, "begin")

    def first(i):
        return functools.partial(scatter, i, "first")

    def second(i):
        return functools.partial(scatter, i, "second")

    def third(i):
        return functools.partial(scatter, i, "third")

    before = [
        [few_plane.second, few_plane.third, few_plane.finish, planes[0].third, planes[1].second],
        [line.second, planes[2].first, planes[1].third],
        [line.third, planes[3].first, planes[2].second, begin(0)],
        [planes[2].third, planes[3].second, first(0)],
        [planes[3].third, second(0), begin(1)],
        [third(0), first(1)],
        [second(1), begin(2)],
        [third(1), first(2)],
    ]
    after = [begin(3), second(2), first(3), third(2), second(3), third(3)]

    planes[0].second()
    line.first()
    planes[1].first()
    arrived(0)
    for copy in loads(0):
        copy.start()
    for copy in weights:
        copy.wait()

    @pl.loop(0, STEPS)
    def _(step):
        for number in range(STEPS):

            @pl.when(step == number)
            def _():
                for action in before[number]:
                    action()
                if number + 1 < STEPS:
                    arrived(number + 1)

        group, z, y = where(step)
        for b in range(4):
            block = few_all[4 * y + b, z]
            block = jnp.concatenate([block, jnp.zeros((LANES - few_rows, LANES), F32)], axis=0)
            by_buf[pl.ds(b * rows, rows)] = block.T
        for copy in loads(step):
            copy.wait()
        pre_buf[...] = times_back(x_buf[...].reshape(chunk, width), w_both[...])
        back_buf[...] = times_back(g_buf[...].reshape(chunk, width), w_down[...])

        @pl.when(step + 1 < STEPS)
        def _():
            for copy in loads(step + 1):
                copy.start()

        @pl.when(step >= 1)
        def _():
            for copy in stores(step - 1):
                copy.wait()

        size = 32

        @pl.loop(0, chunk // size)
        def _(i):
            at = pl.ds(pl.multiple_of(i * size, size), size)
            gate_pre, up_pre = pre_buf[at, :units], pre_buf[at, units:]
            back = back_buf[at]
            lane = lax.broadcasted_iota(jnp.int32, (size, LANES), 1)
            factor = by_buf[at]
            by_route = jnp.sum(jnp.where(lane == here.c, factor, 0.0), axis=1, keepdims=True)
            by_switch = jnp.sum(jnp.where(lane == PLANE, factor, 0.0), axis=1, keepdims=True)
            is_routed = lax.broadcasted_iota(jnp.int32, (size, units), 1) < routed
            by = jnp.where(is_routed, by_route, by_switch)
            sigma = jax.nn.sigmoid(gate_pre)
            act = gate_pre * sigma
            hidden = act * up_pre
            product = hidden * back
            routed_dot = jnp.sum(jnp.where(is_routed, product, 0.0), axis=1, keepdims=True)
            shared_dot = jnp.sum(jnp.where(is_routed, 0.0, product), axis=1, keepdims=True)
            dot_buf[at] = jnp.where(
                lane == here.c, routed_dot, jnp.where(lane == PLANE, shared_dot, 0.0)
            )
            back = back * by
            block, inner = i // (rows // size), i % (rows // size)
            inside = pl.ds(pl.multiple_of(inner * size, size), size)
            h_buf[block, inside] = (hidden * by).astype(BF16)
            slope = sigma * (1.0 + gate_pre * (1.0 - sigma))
            p_buf[block, inside, :units] = (back * up_pre * slope).astype(BF16)
            p_buf[block, inside, units:] = (back * act).astype(BF16)

        for b in range(4):
            dots_parts[group, 2 * y + b // 2, b % 2] = dot_buf[pl.ds(b * rows, rows)].T[:few_rows]

        @pl.loop(0, width // TILE)
        def _(i):
            at = pl.ds(pl.multiple_of(i * TILE, TILE), TILE)
            both = p_buf[...].reshape(chunk, 2 * units)
            tile = dot(both, w_both[:, at]).astype(BF16)
            parts[group, pl.ds(2 * y, 2), :, :, at] = tile.reshape(2, 2, rows, TILE)
            weighted = h_buf[...].reshape(chunk, units)
            tile = dot(weighted, w_down[:, at]).astype(BF16)
            o_buf[:, :, :, at] = tile.reshape(2, 2, rows, TILE)

        for copy in stores(step):
            copy.start()

    for action in after:
        action()
    for copy in stores(STEPS - 1):
        copy.wait()
    for copy in arrivals:
        copy.wait_recv()
    size = 32

    @pl.loop(0, rows // size)
    def _(i):
        at = pl.ds(pl.multiple_of(i * size, size), size)
        value = jobs[0].mine()[at].astype(F32)
        for j in range(3):
            value += landed[j, at].astype(F32)
        sum_out[at] = value

    dots_out[...] = dots_jobs[0].mine()[...] + dots_landed[0] + dots_landed[1] + dots_landed[2]
    line.finish()
    wire.close()


def feed_forward(x, few, g, mixed, shared, routed_down, shared_down, units):
    rows, width = x.shape
    copies = 3 + LINE_GATHER_COPIES + 5 * PLANE_GATHER_COPIES + 8 * PLANE_SCATTER_COPIES + 12
    return call(
        ffn_kernel,
        2,
        [
            ((LINE, PLANE, rows, width), BF16),
            ((rows, width), F32),
            (few.shape, F32),
            ((LINE, 4, 2, rows, width), BF16),
            ((LINE, PLANE, rows, 2 * units), BF16),
            ((LINE, PLANE, rows, units), BF16),
        ],
        [x, few, g.reshape(LINE, PLANE, rows, width), mixed, shared, routed_down, shared_down],
        wires(copies)
        + [
            pltpu.SemaphoreType.DMA((14,)),
            pltpu.SemaphoreType.DMA((2,)),
            pltpu.SemaphoreType.DMA((3,)),
            pltpu.VMEM((2 * units, width), BF16),
            pltpu.VMEM((units, width), BF16),
            pltpu.VMEM((PLANE, LINE) + few.shape, F32),
            pltpu.VMEM((4, 4, 2, rows, width), BF16),
            pltpu.VMEM((3, rows, width), BF16),
            pltpu.VMEM((4, 4, 2) + few.shape, F32),
            pltpu.VMEM((3,) + few.shape, F32),
            pltpu.VMEM((4, rows, width), BF16),
            pltpu.VMEM((4, rows, width), BF16),
            pltpu.VMEM((2, 2, rows, width), BF16),
            pltpu.VMEM((4, rows, 2 * units), BF16),
            pltpu.VMEM((4, rows, units), BF16),
            pltpu.VMEM((4 * rows, 2 * units), F32),
            pltpu.VMEM((4 * rows, units), F32),
            pltpu.VMEM((4 * rows, LANES), F32),
            pltpu.VMEM((4 * rows, LANES), F32),
        ]
        + scatter_room(rows, width, BF16) * 4
        + scatter_room(few.shape[0], LANES, F32) * 4,
        out_specs=[HBM, VMEM, VMEM, HBM, HBM, HBM],
        in_specs=[VMEM, VMEM] + [HBM] * 5,
    )


def fan_kernel(block, shared, out, shared_out, send, recv, local):
    here, wire = Place(), Wire(send, recv)
    greet(
        [here.plane(c) for c in (here.twin, here.across, here.along)]
        + [here.line(z) for z in here.on_line()]
    )
    half = block.shape[0] // 2
    mine = pltpu.make_async_copy(block, out.at[here.c], local.at[0])
    mine.start()
    jobs = []
    for i in range(2):
        at = pl.ds(i * half, half)
        jobs.append(
            PlaneGather(
                wire, here, functools.partial(lambda at, c: out.at[c, at], at), block.at[at]
            ).first()
        )
    kept = pltpu.make_async_copy(shared.at[:, here.z], shared_out.at[here.z], local.at[1])
    kept.start()
    moved = [
        wire.push(shared.at[:, z], shared_out.at[here.z], here.line(z)) for z in here.on_line()
    ]
    for job in jobs:
        job.second()
    for job in jobs:
        job.third()
    for job in jobs:
        job.finish()
    for copy in moved:
        copy.wait_recv()
    kept.wait()
    mine.wait()
    wire.close()


def fan_plane(block, shared):
    out, shared = call(
        fan_kernel,
        5,
        [((PLANE,) + block.shape, block.dtype), ((LINE, PLANE) + shared.shape[2:], BF16)],
        [block, shared],
        wires(2 * PLANE_GATHER_COPIES + 3) + [pltpu.SemaphoreType.DMA((2,))],
        in_specs=[VMEM, HBM],
    )
    return out.reshape(PLANE * block.shape[0], block.shape[1]), shared


def end_kernel(
    parts, ffn, three, output, shared, bias, terms,
    out, ffn_out, three_out, output_out, shared_out, bias_out, terms_out,
    send, recv, local, held, ffn_held, three_held, output_held, *rooms
):
    here, wire = Place(), Wire(send, recv)
    room, ffn_rooms = rooms[:5], [rooms[5 + 5 * i : 10 + 5 * i] for i in range(4)]
    ffn_room, three_room, output_room = rooms[25:27], rooms[27:29], rooms[29:31]
    terms_in, terms_own, terms_line = rooms[31:]
    others = [(here.c + step) % PLANE for step in range(1, PLANE)]
    greet([here.plane(c) for c in others] + [here.line(z) for z in here.on_line()])
    on_line = here.on_line()
    places = [here.mirrored(i) for i in (2, 3, 1, 0)]
    loads = [
        pltpu.make_async_copy(three.at[:, z], three_held.at[z], local.at[z]) for z in range(LINE)
    ]
    loads += [
        pltpu.make_async_copy(parts, held, local.at[4]),
        pltpu.make_async_copy(output, output_held, local.at[5]),
        pltpu.make_async_copy(terms.at[here.c], terms_own, local.at[6]),
        pltpu.make_async_copy(bias, bias_out.at[here.z], local.at[7]),
    ]
    shared_own = pltpu.make_async_copy(shared.at[:, here.c], shared_out.at[here.c], local.at[8])
    shared_own.start()
    loads += [
        pltpu.make_async_copy(ffn.at[z], ffn_held.at[i], local.at[9 + i])
        for i, z in enumerate(places)
    ]
    for copy in loads:
        copy.start()
    job = PlaneScatter(wire, here, held, room)
    ffn_jobs = [PlaneScatter(wire, here, ffn_held.at[i], ffn_rooms[i]) for i in range(4)]
    three_line = LineScatter(
        wire, here, [three_held.at[here.mirrored(i)] for i in range(4)], three_room
    )
    output_line = LineScatter(
        wire, here, [output_held.at[here.mirrored(i)] for i in range(4)], output_room
    )
    ffn_line = LineScatter(wire, here, [ffn_jobs[i].mine() for i in (3, 2, 0, 1)], ffn_room)
    for copy in loads[:4]:
        copy.wait()
    three_line.begin()
    loads[4].wait()
    job.begin()
    for copy in loads[5:]:
        copy.wait()
    terms_plane = [
        wire.push(terms.at[c], terms_in.at[j], here.plane(c)) for j, c in enumerate(others)
    ]
    shared_plane = [
        wire.push(shared.at[:, c], shared_out.at[here.c], here.plane(c)) for c in others
    ]
    bias_line = [wire.push(bias, bias_out.at[here.z], here.line(z)) for z in on_line]
    ffn_jobs[0].begin()
    ffn_jobs[1].begin()
    job.first()
    output_line.begin()
    ffn_jobs[0].first()
    job.second()
    ffn_jobs[2].begin()
    ffn_jobs[1].first()
    ffn_jobs[0].second()
    for copy in terms_plane:
        copy.wait_recv()
    total = terms_own[...]
    for j in range(PLANE - 1):
        total += terms_in[j]
    terms_own[...] = total
    terms_last = [
        wire.push(terms_own.at[z], terms_line.at[j], here.line(z)) for j, z in enumerate(on_line)
    ]
    three_line.first()
    job.third()
    out[...] = job.mine()[...].astype(F32)
    ffn_jobs[3].begin()
    ffn_jobs[2].first()
    ffn_jobs[1].second()
    ffn_jobs[0].third()
    ffn_jobs[3].first()
    ffn_jobs[2].second()
    ffn_jobs[1].third()
    three_line.second()
    ffn_jobs[3].second()
    ffn_jobs[2].third()
    ffn_line.begin()
    output_line.first()
    ffn_jobs[3].third()
    three_line.third()
    three_plane = [
        wire.push(three_held.at[here.z, c], three_out.at[here.c], here.plane(c)) for c in others
    ]
    kept = pltpu.make_async_copy(three_held.at[here.z, here.c], three_out.at[here.c], local.at[0])
    kept.start()
    ffn_line.first()
    output_line.second()
    ffn_line.second()
    output_line.third()
    output_out[...] = output_held[here.z].astype(F32)
    for copy in terms_last:
        copy.wait_recv()
    terms_out[...] = terms_own[here.z] + terms_line[0] + terms_line[1] + terms_line[2]
    ffn_line.third()
    ffn_out[...] = ffn_held[3 - here.depth, here.y * 2 + here.x, here.core].astype(F32)
    for copy in bias_line + shared_plane + three_plane:
        copy.wait_recv()
    kept.wait()
    shared_own.wait()
    wire.close()


def line_room(shape, kind):
    return [pltpu.VMEM((3,) + shape, kind), pltpu.VMEM((2,) + shape, kind)]


def end_transfers(parts, ffn, three, output, shared, bias, terms):
    rows, width = parts.shape[0] // PLANE, parts.shape[1]
    _, _, owned, wide = three.shape
    copies = 5 * PLANE_SCATTER_COPIES + 3 * LINE_SCATTER_COPIES + 3 + 7 + 3 + 7 + 7
    return call(
        end_kernel,
        6,
        [
            ((rows, width), F32),
            ((rows, width), F32),
            ((PLANE, owned, wide), BF16),
            ((owned, width), F32),
            ((PLANE, LINE) + shared.shape[2:], BF16),
            ((LINE,) + bias.shape, F32),
            (terms.shape[2:], F32),
        ],
        [parts.reshape(4, 2, rows, width), ffn, three, output, shared, bias, terms],
        wires(copies)
        + [
            pltpu.SemaphoreType.DMA((13,)),
            pltpu.VMEM((4, 2, rows, width), BF16),
            pltpu.VMEM((LINE, 4, 2, rows, width), BF16),
            pltpu.VMEM((LINE, PLANE, owned, wide), BF16),
            pltpu.VMEM((LINE, owned, width), BF16),
        ]
        + scatter_room(rows, width, BF16) * 5
        + line_room((rows, width), BF16)
        + line_room((PLANE, owned, wide), BF16)
        + line_room((owned, width), BF16)
        + [
            pltpu.VMEM((PLANE - 1,) + terms.shape[1:], F32),
            pltpu.VMEM(terms.shape[1:], F32),
            pltpu.VMEM((3,) + terms.shape[2:], F32),
        ],
        out_specs=[VMEM, VMEM, HBM, VMEM, HBM, HBM, VMEM],
        in_specs=[HBM] * 5 + [VMEM, HBM],
    )


def rms_scale(values):
    return lax.rsqrt(jnp.mean(values * values, axis=-1, keepdims=True) + EPS)


def rope_tables(places, head_size):
    half = head_size // 2
    freqs = jnp.exp(jnp.arange(half, dtype=F32) * (-2.0 * math.log(ROPE_BASE) / head_size))
    angles = places.astype(F32)[:, None] * freqs[None, :]
    return (jnp.cos(angles)[:, None, :], jnp.sin(angles)[:, None, :])


def rotate(values, cosine, sine):
    half = values.shape[-1] // 2
    first = values[..., :half]
    second = values[..., half:]
    return jnp.concatenate(
        [first * cosine - second * sine, second * cosine + first * sine], axis=-1
    )


def dot(left, right):
    return jnp.dot(left, right, preferred_element_type=F32)


def times_back(left, right):
    return lax.dot_general(left, right, (((1,), (1,)), ((), ())), preferred_element_type=F32)


def outer_sum(left, right):
    return lax.dot_general(left, right, (((0,), (0,)), ((), ())), preferred_element_type=F32)


def gather_plane(shard):
    return lax.all_gather(shard, "ctx", axis=0, tiled=True)


def scatter_plane(partial):
    return lax.psum_scatter(partial, "ctx", scatter_dimension=0, tiled=True)


def scatter_line(partial):
    return lax.psum_scatter(partial, "fsdp", scatter_dimension=0, tiled=False)


def over(step, carry, items, unrolled):
    if not unrolled:
        return lax.scan(step, carry, items)
    outs = []
    for i in range(jax.tree.leaves(items)[0].shape[0]):
        carry, out = step(carry, jax.tree.map(lambda item: item[i], items))
        outs.append(out)
    return carry, jax.tree.map(lambda *parts: jnp.stack(parts), *outs)


def blocks(length):
    return length // min(length, BLOCK)


def cut(array, axis=0):
    shape = array.shape
    count = blocks(shape[axis])
    shape = shape[:axis] + (count, shape[axis] // count) + shape[axis + 1 :]
    return jnp.moveaxis(array.reshape(shape), axis, 0)


def attend(queries, keys, values, starts):
    length = queries.shape[0]
    scale = 1.0 / math.sqrt(HEAD)
    cols = jnp.arange(length, dtype=jnp.int32)[None, :]

    def step(carry, items):
        part, low, rows = items
        mask = ((cols <= rows[:, None]) & (cols >= low[:, None]))[None]
        scores = jnp.einsum("qhd,khd->hqk", part, keys, preferred_element_type=F32)
        scores = jnp.where(mask, scores * scale, MASKED)
        best = jnp.max(scores, axis=-1, keepdims=True)
        weights = jnp.exp(scores - best)
        total = jnp.sum(weights, axis=-1, keepdims=True)
        probs = (weights / total).astype(BF16)
        out = jnp.einsum("hqk,khd->qhd", probs, values, preferred_element_type=F32)
        return carry, (out, best + jnp.log(total))

    items = (cut(queries), cut(starts), cut(cols[0]))
    _, (outs, logs) = over(step, 0, items, blocks(length) == 1)
    return outs.reshape(queries.shape), jnp.moveaxis(logs, 0, 1).reshape(-1, length, 1)


def attend_back(queries, keys, values, starts, logs, grad_attn, delta):
    length = queries.shape[0]
    scale = 1.0 / math.sqrt(HEAD)
    cols = jnp.arange(length, dtype=jnp.int32)[None, :]

    def step(carry, items):
        grad_keys, grad_values = carry
        part, low, rows, log, grad, less = items
        mask = ((cols <= rows[:, None]) & (cols >= low[:, None]))[None]
        scores = jnp.einsum("qhd,khd->hqk", part, keys, preferred_element_type=F32)
        probs = jnp.where(mask, jnp.exp(scores * scale - log), 0.0)
        grad_probs = jnp.einsum("qhd,khd->hqk", grad, values, preferred_element_type=F32)
        grad_scores = (probs * (grad_probs - less[:, :, None])).astype(BF16)
        grad_queries = scale * jnp.einsum(
            "hqk,khd->qhd", grad_scores, keys, preferred_element_type=F32
        )
        grad_keys += scale * jnp.einsum(
            "hqk,qhd->khd", grad_scores, part, preferred_element_type=F32
        )
        grad_values += jnp.einsum(
            "hqk,qhd->khd", probs.astype(BF16), grad, preferred_element_type=F32
        )
        return (grad_keys, grad_values), grad_queries

    zeros = jnp.zeros(keys.shape, F32)
    items = (cut(queries), cut(starts), cut(cols[0]), cut(logs, 1), cut(grad_attn), cut(delta, 1))
    carry, grad_queries = over(step, (zeros, zeros), items, blocks(length) == 1)
    return grad_queries.reshape(queries.shape), carry[0], carry[1]


def body(
    tokens,
    positions,
    routes,
    cotangent,
    attn_gain,
    query_weight,
    key_weight,
    value_weight,
    query_bias,
    key_bias,
    value_bias,
    output_weight,
    ffn_gain,
    router_weight,
    expert_gate,
    expert_up,
    expert_down,
    shared_gate,
    shared_up,
    shared_down,
    shared_sigmoid,
):
    plane, line = lax.axis_size("ctx"), lax.axis_size("fsdp")
    place = lax.axis_index("ctx")
    rows, width = tokens.shape[1], tokens.shape[2]
    length = plane * rows
    experts = router_weight.shape[1]
    groups = math.gcd(HEADS, plane)
    share = plane // groups
    heads = HEADS // groups
    span = heads * HEAD
    owned = width // (plane * line)
    group = place // share

    fast = (plane, line) == (PLANE, LINE) and share == 1
    three = jnp.stack([query_weight, key_weight, value_weight])
    routed_units, shared_units = expert_down.shape[1], shared_down.shape[0]
    columns = [attn_gain, query_bias, key_bias, value_bias, ffn_gain, shared_sigmoid]
    columns = jnp.concatenate([jnp.stack(columns, axis=1), router_weight], axis=1)
    x_own, g_own = tokens[0], cotangent[0]
    shared = [w.reshape(owned, plane * line, shared_units) for w in (shared_gate, shared_up)]
    shared = jnp.concatenate(shared, axis=2).transpose(1, 0, 2)
    routed = jnp.stack([expert_gate[0].T, expert_up[0].T]).reshape(2, line, routed_units, -1)
    routed = routed.transpose(1, 0, 2, 3)
    if fast:
        high, low = positions[0] // 64, positions[0] % 64
        digits = jnp.stack([high, low]).reshape(2 * (rows // owned), owned).T.astype(BF16)
        small = jnp.concatenate([columns, digits], axis=1)
        marks = small.shape[1]
        small = jnp.pad(small, ((0, 0), (0, LANES - marks)))
        sent = three.reshape(3, owned, plane, span).transpose(2, 1, 0, 3)
        x_all, w_three, w_output, small, shared, g_sent = start_transfers(
            x_own,
            sent.reshape(plane, owned, 3 * span),
            output_weight,
            small,
            shared.reshape(plane, line, owned, 2 * shared_units),
            g_own,
        )
        routed = routed.reshape(line, 2 * routed_units, -1)
        routed = lax.all_to_all(routed, "fsdp", split_axis=0, concat_axis=0, tiled=True)
        x_all = x_all.reshape(length, width)
        w_three = w_three.reshape(width, 3 * span)
        w_output = w_output.reshape(span, width)
        digits = lax.dynamic_index_in_dim(small, lax.axis_index("fsdp"), 1, keepdims=False)
        digits = digits[:, :, columns.shape[1] : marks].astype(jnp.int32)
        digits = digits.transpose(0, 2, 1).reshape(plane, 2, rows)
        places = (digits[:, 0] * 64 + digits[:, 1]).reshape(length)
        small = small.reshape(width, LANES)[:, : columns.shape[1]]
        g_all = lax.all_gather(g_sent, ("fsdp", "ctx"), axis=0, tiled=True)
    else:
        small = lax.all_gather(columns, BOTH, axis=0, tiled=True)
        places = lax.all_gather(positions[0], "ctx", axis=0, tiled=True)
        x_all = gather_plane(x_own)
        whole = lax.all_gather(three, BOTH, axis=1, tiled=True)
        whole = lax.dynamic_slice_in_dim(whole, group * span, span, 2)
        w_three = whole.transpose(1, 0, 2).reshape(width, 3 * span)
        w_output = lax.all_gather(output_weight, BOTH, axis=0, tiled=True)
        w_output = lax.dynamic_slice_in_dim(w_output, group * span, span, 0)
    gain_in = small[:, 0].astype(F32)
    gain_mid = small[:, 4].astype(F32)
    w_switch = small[:, 5]
    w_router = small[:, 6:]
    biases = lax.dynamic_slice_in_dim(small[:, 1:4], group * span, span, 0).astype(F32)
    biases = biases.T.reshape(3 * span)
    used = routed_units + shared_units
    units = -(-used // LANES) * LANES

    states = x_all.astype(F32)
    starts = jnp.arange(length, dtype=jnp.int32) - places
    unit_in = states * rms_scale(states)
    normed = (unit_in * gain_in[None, :]).astype(BF16)
    cosine, sine = rope_tables(places, HEAD)
    pre = (dot(normed, w_three) + biases[None, :]).reshape(length, 3, heads, HEAD)
    queries = rotate(pre[:, 0], cosine, sine).astype(BF16)
    keys = rotate(pre[:, 1], cosine, sine).astype(BF16)
    values = pre[:, 2].astype(BF16)
    attn_rows, logs = attend(queries, keys, values, starts)
    if share > 1:
        mine = jnp.arange(length, dtype=jnp.int32) // (length // share) == place % share
        attn_rows = jnp.where(mine[:, None, None], attn_rows, 0.0)
    attn_low = attn_rows.reshape(length, span).astype(BF16)
    branch = dot(attn_low, w_output).astype(BF16)
    if fast:
        branch, shared = fold_plane(branch, shared)
    else:
        branch = scatter_plane(branch).astype(F32)
    mid = x_own.astype(F32) + branch

    scale_mid = rms_scale(mid)
    unit_mid = mid * scale_mid
    normed2 = (unit_mid * gain_mid[None, :]).astype(BF16)
    router_probs = jax.nn.softmax(dot(normed2, w_router), axis=-1)
    picks = routes[0][:, :, None] == jnp.arange(experts, dtype=jnp.int32)[None, None, :]
    hits = jnp.any(picks, axis=1)
    switch = jax.nn.sigmoid(dot(normed2, w_switch[:, None]))
    factors = jnp.concatenate([jnp.where(hits, router_probs, 0.0), switch], axis=1)
    mine = jnp.arange(experts, dtype=jnp.int32) == place

    def hidden_units(x_all, g_all, by_route, by_switch, w_both, w_down):
        number = jnp.arange(units, dtype=jnp.int32)
        by = jnp.where(number < routed_units, by_route[:, None], by_switch[:, None])
        pre = times_back(x_all, w_both)
        gate_pre, up_pre = pre[:, :units], pre[:, units:]
        grad_hidden = times_back(g_all, w_down)
        sigma = jax.nn.sigmoid(gate_pre)
        act = gate_pre * sigma
        hidden = act * up_pre
        product = hidden * grad_hidden
        routed_dot = jnp.sum(product[:, :routed_units], axis=1)
        shared_dot = jnp.sum(product[:, routed_units:used], axis=1)
        weighted = (hidden * by).astype(BF16)
        slope = sigma * (1.0 + gate_pre * (1.0 - sigma))
        grad_hidden = grad_hidden * by
        grad_pre = jnp.concatenate([grad_hidden * up_pre * slope, grad_hidden * act], axis=1)
        grad_pre = grad_pre.astype(BF16)
        grad_part = dot(grad_pre, w_both).astype(BF16)
        out_part = dot(weighted, w_down).astype(BF16)
        terms = (outer_sum(grad_pre, x_all), outer_sum(weighted, g_all))
        return terms, out_part, grad_part, routed_dot, shared_dot

    def units_of(routed, shared, spare):
        return jnp.concatenate([routed[0], shared[0], spare, routed[1], shared[1], spare], axis=0)

    def parts_of(term):
        routed = [term[:routed_units], term[units : units + routed_units]]
        shared = [term[routed_units:used], term[units + routed_units : units + used]]
        return jnp.stack(routed), jnp.stack(shared)

    if fast:
        few = jnp.pad(factors.T, ((0, 16 - experts - 1), (0, 0)))
        shared = shared.reshape(width, 2 * shared_units).T
        x_all, grad_ffn, dots, out_part, grad_pre, weighted = feed_forward(
            normed2, few, g_all, routed, shared, expert_down[0], shared_down, units
        )
        term_both = outer_sum(
            grad_pre.reshape(line * length, 2 * units), x_all.reshape(line * length, width)
        )
        term_down = outer_sum(weighted.reshape(line * length, units), g_all)
        routed, shared = parts_of(term_both.astype(BF16))
        routed = routed.reshape(2 * routed_units, line, -1).transpose(1, 0, 2)
        routed = lax.all_to_all(routed, "fsdp", split_axis=0, concat_axis=0, tiled=True)
        routed = routed.reshape(line, 2, routed_units, -1)
        shared = shared.reshape(2 * shared_units, width).T
        shared = shared.reshape(plane, line, owned, 2 * shared_units)
        dots = dots[: experts + 1].T
    else:
        routed = lax.all_to_all(routed, "fsdp", split_axis=0, concat_axis=0, tiled=True)
        routed = routed.transpose(1, 2, 0, 3).reshape(2, routed_units, width)
        spare = jnp.zeros((units - used, width), BF16)
        w_down = jnp.concatenate([expert_down[0], shared_down, spare], axis=0)
        factors = lax.all_gather(factors, ("fsdp", "ctx"), axis=0, tiled=True)
        factors = factors.reshape(line, length, experts + 1)
        x_line = lax.all_gather(normed2, "fsdp", axis=0, tiled=False)
        g_line = lax.all_gather(g_own, "fsdp", axis=0, tiled=False)

        shared = lax.all_to_all(shared, BOTH, split_axis=0, concat_axis=0, tiled=True)
        shared = shared.reshape(width, 2, shared_units).transpose(1, 2, 0)
        w_both = units_of(routed, shared, spare)

        def step(terms, items):
            x_part, g_part, factor = items
            by_route = jnp.sum(jnp.where(mine, factor[:, :experts], 0.0), axis=1)
            more, out_part, grad_part, routed_dot, shared_dot = hidden_units(
                gather_plane(x_part), gather_plane(g_part), by_route, factor[:, experts], w_both, w_down
            )
            dots = jnp.where(mine, routed_dot[:, None], 0.0)
            dots = jnp.concatenate([dots, shared_dot[:, None]], axis=1)
            terms = tuple(term + part for term, part in zip(terms, more))
            return terms, (scatter_plane(out_part), scatter_plane(grad_part), dots)

        terms = tuple(jnp.zeros(w.shape, F32) for w in (w_both, w_down))
        terms, (out_parts, grad_parts, dots) = lax.scan(step, terms, (x_line, g_line, factors))
        term_both, term_down = terms
        grad_ffn = scatter_line(grad_parts).astype(F32)
        ffn = scatter_line(out_parts).astype(F32)
        dots = dots.reshape(line, plane, rows, experts + 1)
        dots = lax.psum_scatter(dots, "ctx", scatter_dimension=1, tiled=False)
        dots = scatter_line(dots)

        routed, shared = parts_of(term_both.astype(BF16))
        grad_shared_gate, grad_shared_up = [
            lax.all_to_all(t.T, BOTH, split_axis=0, concat_axis=1, tiled=True).astype(F32)
            for t in shared
        ]
        routed = routed.reshape(2, routed_units, line, -1).transpose(2, 0, 1, 3)
        routed = lax.all_to_all(routed, "fsdp", split_axis=0, concat_axis=0, tiled=True)
    grad_expert_down = term_down[:routed_units][None]
    grad_shared_down = term_down[routed_units:used]

    grad_out = cotangent[0].astype(F32)
    grad_probs = jnp.where(hits, dots[:, :experts], 0.0)
    grad_logits = (
        router_probs * (grad_probs - jnp.sum(router_probs * grad_probs, axis=-1, keepdims=True))
    ).astype(BF16)
    grad_switch = dots[:, experts:] * switch * (1.0 - switch)
    grad_normed2 = (
        grad_ffn + times_back(grad_logits, w_router) + grad_switch * w_switch.astype(F32)[None, :]
    )
    scaled_mid = grad_normed2 * gain_mid[None, :]
    grad_mid = grad_out + scale_mid * (
        scaled_mid - unit_mid * jnp.mean(scaled_mid * unit_mid, axis=-1, keepdims=True)
    )
    terms = jnp.concatenate(
        [
            jnp.sum(grad_normed2 * unit_mid, axis=0)[:, None],
            jnp.sum(grad_switch * normed2.astype(F32), axis=0)[:, None],
            outer_sum(normed2, grad_logits),
        ],
        axis=1,
    )

    grad_branch = grad_mid.astype(BF16)
    if fast:
        grad_branch, shared = fan_plane(grad_branch, shared)
    else:
        grad_branch = gather_plane(grad_branch)
    routed = routed.transpose(1, 3, 0, 2).reshape(2, 1, -1, line * routed_units).astype(F32)
    grad_attn = times_back(grad_branch, w_output).reshape(length, heads, HEAD).astype(BF16)
    if share > 1:
        mine = jnp.arange(length, dtype=jnp.int32) // (length // share) == place % share
        grad_attn = jnp.where(mine[:, None, None], grad_attn, 0)
    delta = jnp.sum(grad_attn.astype(F32) * attn_rows, axis=-1).T
    grad_queries, grad_keys, grad_values = attend_back(
        queries, keys, values, starts, logs, grad_attn, delta
    )
    grad_pre = jnp.concatenate(
        [
            rotate(grad_queries, cosine, -sine).reshape(length, span),
            rotate(grad_keys, cosine, -sine).reshape(length, span),
            grad_values.reshape(length, span),
        ],
        axis=1,
    ).astype(BF16)
    grad_part = times_back(grad_pre, w_three).astype(BF16)
    term_three = outer_sum(normed, grad_pre)
    term_output = outer_sum(attn_low, grad_branch)
    term_bias = jnp.sum(grad_pre.astype(F32), axis=0)
    if fast:
        count = terms.shape[1]
        terms = terms.reshape(plane, line, owned * count)
        terms = jnp.pad(terms, ((0, 0), (0, 0), (0, 8 * LANES - owned * count)))
        grad_normed, ffn, grad_three, grad_output, shared, term_bias, terms = end_transfers(
            grad_part,
            out_part,
            term_three.astype(BF16).reshape(plane, line, owned, 3 * span),
            term_output.astype(BF16).reshape(line, owned, width),
            shared,
            jnp.broadcast_to(term_bias[None], (8, 3 * span)),
            terms.reshape(plane, line, 8, LANES),
        )
        grad_three = grad_three.reshape(plane, owned, 3, span).transpose(2, 1, 0, 3)
        grad_three = grad_three.reshape(3, owned, width).astype(F32)
        term_bias = jnp.sum(term_bias[:, 0], axis=0).reshape(3, line, owned)
        grad_bias = lax.dynamic_index_in_dim(term_bias, lax.axis_index("fsdp"), 1, keepdims=False)
        terms = terms.reshape(-1)[: owned * count].reshape(owned, count)
        shared = shared.reshape(plane * line, owned, 2, shared_units).transpose(2, 1, 0, 3)
        shared = shared.reshape(2, owned, -1).astype(F32)
        grad_shared_gate, grad_shared_up = shared[0], shared[1]
    else:
        grad_normed = scatter_plane(grad_part).astype(F32)
        zeros = jnp.zeros((3, width, width), BF16)
        spread = lax.dynamic_update_slice_in_dim(
            zeros, term_three.astype(BF16).reshape(width, 3, span).transpose(1, 0, 2), group * span, 2
        )
        grad_three = lax.psum_scatter(spread, BOTH, scatter_dimension=1, tiled=True).astype(F32)
        spread = lax.dynamic_update_slice_in_dim(
            zeros[0], term_output.astype(BF16), group * span, 0
        )
        grad_output = lax.psum_scatter(spread, BOTH, scatter_dimension=0, tiled=True).astype(F32)
        spread = lax.dynamic_update_slice_in_dim(
            jnp.zeros((3, width), F32), term_bias.reshape(3, span), group * span, 1
        )
        grad_bias = lax.psum_scatter(spread, BOTH, scatter_dimension=1, tiled=True)
        terms = lax.psum_scatter(terms, BOTH, scatter_dimension=0, tiled=True)
    grad_attn_gain = jnp.sum(three.astype(F32) * grad_three, axis=(0, 2)) / attn_gain.astype(F32)
    own_states = tokens[0].astype(F32)
    scale_in = rms_scale(own_states)
    own_unit = own_states * scale_in
    scaled_in = grad_normed * gain_in[None, :]
    grad_states = grad_mid + scale_in * (
        scaled_in - own_unit * jnp.mean(scaled_in * own_unit, axis=-1, keepdims=True)
    )
    return (
        (mid + ffn).astype(BF16)[None],
        grad_states[None],
        grad_attn_gain,
        grad_three[0],
        grad_three[1],
        grad_three[2],
        grad_bias[0],
        grad_bias[1],
        grad_bias[2],
        grad_output,
        terms[:, 0],
        terms[:, 2:],
        routed[0],
        routed[1],
        grad_expert_down,
        grad_shared_gate,
        grad_shared_up,
        grad_shared_down,
        terms[:, 1],
    )


def solution(mesh):
    tokens, flat, both, routed = (
        P("fsdp", "ctx", None),
        P(BOTH),
        P(BOTH, None),
        P("ctx", "fsdp", None),
    )
    weights = (flat, both, both, both, flat, flat, flat, both, flat, both)
    weights += (routed, routed, routed, both, both, both, flat)
    return jax.shard_map(
        body,
        mesh=mesh,
        in_specs=(tokens, P("fsdp", "ctx"), tokens, tokens) + weights,
        out_specs=(tokens, tokens) + weights,
        check_vma=False,
    )
```

```python
import functools
import math

import jax
import jax.numpy as jnp
from jax import lax
from jax.experimental import pallas as pl
from jax.experimental.pallas import tpu as pltpu
from jax.sharding import PartitionSpec as P

HEADS = 16
HEAD = 128
EPS = 1e-06
ROPE_BASE = 1000000.0
MASKED = -1e30
BLOCK = 1024
BOTH = ("ctx", "fsdp")
BF16 = jnp.bfloat16
F32 = jnp.float32


PLANE, LINE = 8, 4
LANES = 128
HBM = pl.BlockSpec(memory_space=pl.ANY)
VMEM = pl.BlockSpec(memory_space=pltpu.VMEM)


class Place:
    def __init__(self):
        self.c = lax.axis_index("ctx")
        self.z = lax.axis_index("fsdp")
        self.core = self.c % 2
        self.x = (self.c // 2) % 2
        self.y = self.c // 4
        self.twin = self.c + 1 - 2 * self.core
        self.across = self.c + 2 - 4 * self.x
        self.along = self.c + 4 - 8 * self.y
        self.far = self.across + 4 - 8 * self.y
        self.upper = self.z // 2
        self.depth = self.z + self.upper * (3 - 2 * self.z)
        self.near = self.z + 1 - 2 * (self.z % 2)
        self.middle = 3 - self.z

    def mirrored(self, number):
        return number + self.upper * (3 - 2 * number)

    def plane(self, c):
        return (c, self.z)

    def line(self, z):
        return (self.c, z)

    def on_line(self):
        return [(self.z + step) % LINE for step in (2, 1, 3)]


class Wire:
    def __init__(self, send, recv):
        self.send, self.recv, self.used, self.open = send, recv, 0, []

    def copy(self, source, target, device, arrival=None):
        number = self.used
        self.used += 1
        return pltpu.make_async_remote_copy(
            src_ref=source,
            dst_ref=target,
            send_sem=self.send.at[number],
            recv_sem=self.recv.at[number if arrival is None else arrival],
            device_id=device,
            device_id_type=pl.DeviceIdType.MESH,
        )

    def later(self, source, target, device, arrival=None):
        copy = self.copy(source, target, device, arrival)
        self.open.append(copy)
        return copy

    def push(self, source, target, device):
        copy = self.later(source, target, device)
        copy.start()
        return copy

    def close(self):
        for copy in self.open:
            copy.wait_send()


def greet(devices):
    barrier = pltpu.get_barrier_semaphore()
    for device in devices:
        pl.semaphore_signal(
            barrier, inc=1, device_id=device, device_id_type=pl.DeviceIdType.MESH
        )
    pl.semaphore_wait(barrier, len(devices))


class PlaneGather:
    def __init__(self, wire, here, at, source=None):
        source = at(here.c) if source is None else source
        to_x, to_y = here.plane(here.across), here.plane(here.along)
        to_twin = here.plane(here.twin)
        x_block, y_block, far_block = at(here.across), at(here.along), at(here.far)
        half = x_block.shape[0] // 2
        high, low = x_block.at[pl.ds(half, half)], y_block.at[pl.ds(0, half)]
        self.from_x = wire.later(source, at(here.c), to_x)
        self.from_y = wire.later(source, at(here.c), to_y)
        self.far_y = wire.later(high, high, to_y)
        self.far_x = wire.later(low, low, to_x)
        blocks = [(source, at(here.c))] + [(b, b) for b in (x_block, y_block, far_block)]
        self.twins = [wire.later(block, target, to_twin) for block, target in blocks]

    def first(self):
        self.from_x.start()
        self.from_y.start()
        self.twins[0].start()
        return self

    def second(self):
        self.from_x.wait_recv()
        self.far_y.start()
        self.twins[1].start()
        self.from_y.wait_recv()
        self.far_x.start()
        self.twins[2].start()

    def third(self):
        self.far_x.wait_recv()
        self.far_y.wait_recv()
        self.twins[3].start()

    def finish(self):
        for copy in self.twins:
            copy.wait_recv()


PLANE_GATHER_COPIES = 8


class LineGather:
    def __init__(self, wire, here, at, source=None):
        self.wire, self.here, self.at = wire, here, at
        source = at(here.z) if source is None else source
        self.one = wire.push(source, at(here.z), here.line(here.near))
        inner = here.depth == 1
        middle, near = here.line(here.middle), here.line(here.near)
        own, mine = source, at(here.z)
        end, two, three = at(here.mirrored(0)), at(here.mirrored(2)), at(here.mirrored(3))
        self.inner = inner
        self.two_in = wire.copy(own, mine, middle)
        self.three_in = wire.copy(end, end, middle)
        self.two_out = wire.copy(two, two, near)
        self.three_out = wire.copy(three, three, near)

        @pl.when(inner)
        def _():
            self.two_in.start()

    def first(self):
        self.one.wait_recv()
        pl.when(self.inner)(self.three_in.start)

    def second(self):
        @pl.when(self.inner)
        def _():
            self.two_in.wait_recv()
            self.two_out.start()

        @pl.when(self.here.depth == 0)
        def _():
            self.two_out.wait_recv()

    def third(self):
        @pl.when(self.inner)
        def _():
            self.three_in.wait_recv()
            self.three_out.start()

        @pl.when(self.here.depth == 0)
        def _():
            self.three_out.wait_recv()

    def order(self):
        here = self.here
        return [here.z, here.near, here.mirrored(2), here.mirrored(3)]

    def finish(self):
        @pl.when(self.inner)
        def _():
            for copy in (self.two_in, self.three_in, self.two_out, self.three_out):
                copy.wait_send()


LINE_GATHER_COPIES = 5


def add_into(total, part):
    rows = total.shape[0]
    step = min(rows, 32)

    @pl.loop(0, rows // step)
    def _(i):
        at = pl.ds(pl.multiple_of(i * step, step), step)
        total[at] = total[at] + part[at]


class PlaneScatter:
    def __init__(self, wire, here, parts, room):
        self.here, self.parts, self.room = here, parts, room
        arrived, one_x, one_y, two_x, two_y = room
        self.half = arrived.shape[1] // 2
        to_x, to_y = here.plane(here.across), here.plane(here.along)
        self.twin = wire.later(parts.at[:, 1 - here.core], arrived, here.plane(here.twin))
        self.from_x = [
            wire.later(self.block(y, 1 - here.x, 0), one_x.at[y], to_x) for y in range(2)
        ]
        self.from_y = [
            wire.later(self.block(1 - here.y, x, 1), one_y.at[x], to_y) for x in range(2)
        ]
        self.last_y = wire.later(self.block(1 - here.y, here.x, 0), two_y, to_y)
        self.last_x = wire.later(self.block(here.y, 1 - here.x, 1), two_x, to_x)

    def block(self, y, x, half=None):
        if half is None:
            return self.parts.at[y * 2 + x, self.here.core]
        return self.parts.at[y * 2 + x, self.here.core, pl.ds(half * self.half, self.half)]

    def begin(self):
        self.twin.start()

    def first(self):
        self.twin.wait_recv()
        for i in range(4):
            add_into(self.parts.at[i, self.here.core], self.room[0].at[i])
        for copy in self.from_x + self.from_y:
            copy.start()

    def second(self):
        here, one_x, one_y = self.here, self.room[1], self.room[2]
        for copy in self.from_x:
            copy.wait_recv()
        add_into(self.block(1 - here.y, here.x, 0), one_x.at[1 - here.y])
        self.last_y.start()
        for copy in self.from_y:
            copy.wait_recv()
        add_into(self.block(here.y, 1 - here.x, 1), one_y.at[1 - here.x])
        self.last_x.start()
        add_into(self.block(here.y, here.x, 0), one_x.at[here.y])
        add_into(self.block(here.y, here.x, 1), one_y.at[here.x])

    def third(self):
        here, two_x, two_y = self.here, self.room[3], self.room[4]
        self.last_y.wait_recv()
        add_into(self.block(here.y, here.x, 0), two_y)
        self.last_x.wait_recv()
        add_into(self.block(here.y, here.x, 1), two_x)

    def mine(self):
        return self.block(self.here.y, self.here.x)


PLANE_SCATTER_COPIES = 7


class LineScatter:
    def __init__(self, wire, here, blocks, room):
        self.here, self.blocks = here, blocks
        near, middle = here.line(here.near), here.line(here.middle)
        self.ends, self.mids = room
        own = self.blocks
        self.out = [wire.copy(own[i], self.ends.at[k], near) for k, i in enumerate((2, 3, 1))]
        self.over = [wire.copy(own[i], self.mids.at[k], middle) for k, i in enumerate((2, 3))]
        self.home = wire.copy(own[0], self.ends.at[0], near)

    def begin(self):
        @pl.when(self.here.depth == 0)
        def _():
            for copy in self.out:
                copy.start()

    def first(self):
        @pl.when(self.here.depth == 1)
        def _():
            for k in range(2):
                self.out[k].wait_recv()
                add_into(self.blocks[2 + k], self.ends.at[k])
                self.over[k].start()

    def second(self):
        @pl.when(self.here.depth == 1)
        def _():
            self.over[1].wait_recv()
            add_into(self.blocks[0], self.mids.at[1])
            self.home.start()
            self.out[2].wait_recv()
            add_into(self.blocks[1], self.ends.at[2])
            self.over[0].wait_recv()
            add_into(self.blocks[1], self.mids.at[0])

    def third(self):
        @pl.when(self.here.depth == 0)
        def _():
            self.home.wait_recv()
            add_into(self.blocks[0], self.ends.at[0])
            for copy in self.out:
                copy.wait_send()

        @pl.when(self.here.depth == 1)
        def _():
            for copy in self.over + [self.home]:
                copy.wait_send()


LINE_SCATTER_COPIES = 6


def scatter_room(rows, columns, kind):
    half = rows // 2
    return [
        pltpu.VMEM((4, rows, columns), kind),
        pltpu.VMEM((2, half, columns), kind),
        pltpu.VMEM((2, half, columns), kind),
        pltpu.VMEM((half, columns), kind),
        pltpu.VMEM((half, columns), kind),
    ]


def wires(count):
    return [pltpu.SemaphoreType.DMA((count,)), pltpu.SemaphoreType.DMA((count,))]


def call(kernel, number, outs, args, scratch, out_specs=None, in_specs=None, aliases=None):
    return pl.pallas_call(
        kernel,
        out_shape=[jax.ShapeDtypeStruct(shape, kind) for shape, kind in outs],
        in_specs=in_specs or [HBM] * len(args),
        out_specs=out_specs or [HBM] * len(outs),
        scratch_shapes=scratch,
        input_output_aliases=aliases or {},
        compiler_params=pltpu.CompilerParams(
            collective_id=number, has_side_effects=True, vmem_limit_bytes=60 << 20
        ),
    )(*args)


def start_kernel(
    tokens, three, output, small, shared, later, x_out, three_out, output_out, small_out,
    shared_out, later_out, send, recv, local
):
    here, wire = Place(), Wire(send, recv)
    others = [(here.c + step) % PLANE for step in range(1, PLANE)]
    greet([here.plane(c) for c in others] + [here.line(z) for z in here.on_line()])
    small_line = [
        wire.push(small, small_out.at[here.c, here.z], here.line(z)) for z in here.on_line()
    ]
    plane = [
        wire.push(three.at[c], three_out.at[here.c, here.z], here.plane(c)) for c in others
    ]
    mine = [
        pltpu.make_async_copy(small, small_out.at[here.c, here.z], local.at[0]),
        pltpu.make_async_copy(three.at[here.c], three_out.at[here.c, here.z], local.at[1]),
        pltpu.make_async_copy(tokens, x_out.at[here.c], local.at[2]),
        pltpu.make_async_copy(output, output_out.at[here.z], local.at[3]),
        pltpu.make_async_copy(shared.at[:, here.z], shared_out.at[here.z], local.at[4]),
    ]
    for copy in mine:
        copy.start()
    x_plane = PlaneGather(wire, here, lambda c: x_out.at[c], tokens).first()
    for copy in mine:
        copy.wait()
    for copy in small_line + plane:
        copy.wait_recv()
    three_line = LineGather(wire, here, lambda z: three_out.at[:, z])
    output_line = LineGather(wire, here, lambda z: output_out.at[z])
    small_plane = PlaneGather(wire, here, lambda c: small_out.at[c]).first()
    moved = [
        wire.push(shared.at[:, z], shared_out.at[here.z], here.line(z)) for z in here.on_line()
    ]
    x_plane.second()
    small_plane.second()
    x_plane.third()
    small_plane.third()
    three_line.first()
    output_line.first()
    three_line.second()
    output_line.second()
    three_line.third()
    output_line.third()
    x_plane.finish()
    small_plane.finish()
    for copy in moved:
        copy.wait_recv()
    three_line.finish()
    output_line.finish()
    wire.close()


def start_transfers(tokens, three, output, small, shared, later):
    rows, width = tokens.shape
    _, owned, wide = three.shape
    copies = 3 + 7 + 3 + 2 * PLANE_GATHER_COPIES + 2 * LINE_GATHER_COPIES
    return call(
        start_kernel,
        1,
        [
            ((PLANE, rows, width), BF16),
            ((PLANE, LINE, owned, wide), BF16),
            ((LINE, owned, width), BF16),
            ((PLANE, LINE) + small.shape, BF16),
            ((LINE, PLANE) + shared.shape[2:], BF16),
            (later.shape, later.dtype),
        ],
        [tokens, three, output, small, shared, later],
        wires(copies) + [pltpu.SemaphoreType.DMA((5,))],
        in_specs=[VMEM] * 5 + [HBM],
        aliases={5: 5},
    )


def fold_kernel(parts, shared, out, shared_out, *scratch):
    here, wire = Place(), Wire(scratch[0], scratch[1])
    local = scratch[2]
    others = [(here.c + step) % PLANE for step in range(1, PLANE)]
    greet([here.plane(c) for c in others])
    kept = pltpu.make_async_copy(shared.at[:, here.c], shared_out.at[here.c], local.at[2])
    kept.start()
    half = parts.shape[2] // 2
    jobs, loads = [], []
    for i in range(2):
        held, room = scratch[3 + 6 * i], scratch[4 + 6 * i : 9 + 6 * i]
        loads.append(
            pltpu.make_async_copy(parts.at[:, :, pl.ds(i * half, half)], held, local.at[i])
        )
        loads[i].start()
        jobs.append(PlaneScatter(wire, here, held, room))
    for load, job in zip(loads, jobs):
        load.wait()
        job.begin()
    moved = [wire.push(shared.at[:, c], shared_out.at[here.c], here.plane(c)) for c in others]
    for job in jobs:
        job.first()
    for job in jobs:
        job.second()
    for i, job in enumerate(jobs):
        job.third()
        out[pl.ds(i * half, half)] = job.mine()[...].astype(out.dtype)
    for copy in moved:
        copy.wait_recv()
    kept.wait()
    wire.close()


def held_room(rows, columns, kind):
    return [pltpu.VMEM((4, 2, rows, columns), kind)] + scatter_room(rows, columns, kind)


def fold_plane(parts, shared):
    rows, width = parts.shape[0] // PLANE, parts.shape[1]
    return call(
        fold_kernel,
        3,
        [((rows, width), F32), ((PLANE, LINE) + shared.shape[2:], BF16)],
        [parts.reshape(4, 2, rows, width), shared],
        wires(2 * PLANE_SCATTER_COPIES + 7)
        + [pltpu.SemaphoreType.DMA((3,))]
        + held_room(rows // 2, width, BF16) * 2,
        out_specs=[VMEM, HBM],
    )


STEPS, TILE = 8, 512


def ffn_kernel(
    x, few, g, mixed, shared, routed_down, shared_down, x_out, sum_out, dots_out, out_parts, pre_out, weighted_out,
    send, recv, local, fetch, store, w_both, w_down, few_all, parts, landed, dots_parts, dots_landed,
    x_buf, g_buf, o_buf, p_buf, h_buf, pre_buf, back_buf, by_buf, dot_buf, *rooms
):
    here, wire = Place(), Wire(send, recv)
    rows, width = x.shape
    chunk = 4 * rows
    routed, units = routed_down.shape[0], w_down.shape[0]
    used = routed + shared_down.shape[0]
    few_rows = few.shape[0]
    greet(
        [here.plane(c) for c in (here.twin, here.across, here.along)]
        + [here.line(z) for z in here.on_line()]
    )
    own = pltpu.make_async_copy(x, x_out.at[here.z, here.c], local.at[0])
    own.start()
    own_few = pltpu.make_async_copy(few, few_all.at[here.c, here.z], local.at[1])
    own_few.start()
    part = mixed.shape[2]
    pieces = [
        (mixed.at[z, pl.ds(k * routed, routed)], w_both.at[pl.ds(k * units, routed), pl.ds(z * part, part)])
        for z in range(LINE)
        for k in range(2)
    ]
    pieces += [
        (
            shared.at[pl.ds(k * (used - routed), used - routed)],
            w_both.at[pl.ds(k * units + routed, used - routed)],
        )
        for k in range(2)
    ]
    pieces += [
        (routed_down, w_down.at[pl.ds(0, routed)]),
        (shared_down, w_down.at[pl.ds(routed, used - routed)]),
    ]
    weights = [
        pltpu.make_async_copy(source, target, local.at[2 + i])
        for i, (source, target) in enumerate(pieces)
    ]
    for copy in weights:
        copy.start()
    nothing = jnp.zeros((units - used, width), BF16)
    w_both[pl.ds(used, units - used)] = nothing
    w_both[pl.ds(units + used, units - used)] = nothing
    w_down[pl.ds(used, units - used)] = nothing
    few_line = [
        wire.push(few, few_all.at[here.c, here.z], here.line(z)) for z in here.on_line()
    ]
    line = LineGather(wire, here, lambda z: x_out.at[z, here.c], x)
    order = line.order()
    planes = [
        PlaneGather(
            wire, here, functools.partial(lambda z, c: x_out.at[z, c], order[i]), None if i else x
        )
        for i in range(4)
    ]
    few_plane = PlaneGather(wire, here, lambda c: few_all.at[c])
    jobs = [PlaneScatter(wire, here, parts.at[i], rooms[5 * i : 5 * i + 5]) for i in range(4)]
    dots_jobs = [
        PlaneScatter(wire, here, dots_parts.at[i], rooms[20 + 5 * i : 25 + 5 * i])
        for i in range(4)
    ]
    slots = [None, 0, 1 + here.depth, 2 - here.depth]
    base = wire.used
    arrivals = [
        wire.copy(source.at[0, 0, 0], target.at[slot], here.line(here.near))
        for source, target in ((parts, landed), (dots_parts, dots_landed))
        for slot in range(3)
    ]
    lines = [
        wire.later(job.mine(), target.at[slots[i]], here.line(order[i]), base + 3 * k + slots[i])
        for k, (group, target) in enumerate(((jobs, landed), (dots_jobs, dots_landed)))
        for i, job in enumerate(group)
        if i
    ]
    planes[0].first()
    own.wait()
    own_few.wait()
    for copy in few_line:
        copy.wait_recv()
    few_plane.first()

    def where(step):
        group, half = step // 2, step % 2
        late = group // 2
        number = (here.depth + group) % 2 * (1 - late) + group * late
        return group, here.mirrored(number), (here.y + half) % 2

    def loads(step):
        _, z, y = where(step)
        at = pl.ds(4 * y, 4)
        return [
            pltpu.make_async_copy(x_out.at[z, at], x_buf, fetch.at[0]),
            pltpu.make_async_copy(g.at[z, at], g_buf, fetch.at[1]),
        ]

    def stores(step):
        _, z, y = where(step)
        at = pl.ds(4 * y, 4)
        return [
            pltpu.make_async_copy(o_buf, out_parts.at[pl.ds(2 * y, 2), :, z], store.at[0]),
            pltpu.make_async_copy(p_buf, pre_out.at[z, at], store.at[1]),
            pltpu.make_async_copy(h_buf, weighted_out.at[z, at], store.at[2]),
        ]

    def scatter(i, phase):
        for job in (jobs[i], dots_jobs[i]):
            getattr(job, phase)()
        if phase == "third" and i:
            lines[i - 1].start()
            lines[3 + i - 1].start()

    def arrived(step):
        for chip in (0, 1):
            planes[step // 2].twins[step % 2 * 2 + chip].wait_recv()

    def begin(i):
        return functools.partial(scatter, i, "begin")

    def first(i):
        return functools.partial(scatter, i, "first")

    def second(i):
        return functools.partial(scatter, i, "second")

    def third(i):
        return functools.partial(scatter, i, "third")

    before = [
        [few_plane.second, few_plane.third, few_plane.finish, planes[0].third, planes[1].second],
        [line.second, planes[2].first, planes[1].third],
        [line.third, planes[3].first, planes[2].second, begin(0)],
        [planes[2].third, planes[3].second, first(0)],
        [planes[3].third, second(0), begin(1)],
        [third(0), first(1)],
        [second(1), begin(2)],
        [third(1), first(2)],
    ]
    after = [begin(3), second(2), first(3), third(2), second(3), third(3)]

    planes[0].second()
    line.first()
    planes[1].first()
    arrived(0)
    for copy in loads(0):
        copy.start()
    for copy in weights:
        copy.wait()

    @pl.loop(0, STEPS)
    def _(step):
        for number in range(STEPS):

            @pl.when(step == number)
            def _():
                for action in before[number]:
                    action()
                if number + 1 < STEPS:
                    arrived(number + 1)

        group, z, y = where(step)
        for b in range(4):
            block = few_all[4 * y + b, z]
            block = jnp.concatenate([block, jnp.zeros((LANES - few_rows, LANES), F32)], axis=0)
            by_buf[pl.ds(b * rows, rows)] = block.T
        for copy in loads(step):
            copy.wait()
        pre_buf[...] = times_back(x_buf[...].reshape(chunk, width), w_both[...])
        back_buf[...] = times_back(g_buf[...].reshape(chunk, width), w_down[...])

        @pl.when(step + 1 < STEPS)
        def _():
            for copy in loads(step + 1):
                copy.start()

        @pl.when(step >= 1)
        def _():
            for copy in stores(step - 1):
                copy.wait()

        size = 32

        @pl.loop(0, chunk // size)
        def _(i):
            at = pl.ds(pl.multiple_of(i * size, size), size)
            gate_pre, up_pre = pre_buf[at, :units], pre_buf[at, units:]
            back = back_buf[at]
            lane = lax.broadcasted_iota(jnp.int32, (size, LANES), 1)
            factor = by_buf[at]
            by_route = jnp.sum(jnp.where(lane == here.c, factor, 0.0), axis=1, keepdims=True)
            by_switch = jnp.sum(jnp.where(lane == PLANE, factor, 0.0), axis=1, keepdims=True)
            is_routed = lax.broadcasted_iota(jnp.int32, (size, units), 1) < routed
            by = jnp.where(is_routed, by_route, by_switch)
            sigma = jax.nn.sigmoid(gate_pre)
            act = gate_pre * sigma
            hidden = act * up_pre
            product = hidden * back
            routed_dot = jnp.sum(jnp.where(is_routed, product, 0.0), axis=1, keepdims=True)
            shared_dot = jnp.sum(jnp.where(is_routed, 0.0, product), axis=1, keepdims=True)
            dot_buf[at] = jnp.where(
                lane == here.c, routed_dot, jnp.where(lane == PLANE, shared_dot, 0.0)
            )
            back = back * by
            block, inner = i // (rows // size), i % (rows // size)
            inside = pl.ds(pl.multiple_of(inner * size, size), size)
            h_buf[block, inside] = (hidden * by).astype(BF16)
            slope = sigma * (1.0 + gate_pre * (1.0 - sigma))
            p_buf[block, inside, :units] = (back * up_pre * slope).astype(BF16)
            p_buf[block, inside, units:] = (back * act).astype(BF16)

        for b in range(4):
            dots_parts[group, 2 * y + b // 2, b % 2] = dot_buf[pl.ds(b * rows, rows)].T[:few_rows]

        @pl.loop(0, width // TILE)
        def _(i):
            at = pl.ds(pl.multiple_of(i * TILE, TILE), TILE)
            both = p_buf[...].reshape(chunk, 2 * units)
            tile = dot(both, w_both[:, at]).astype(BF16)
            parts[group, pl.ds(2 * y, 2), :, :, at] = tile.reshape(2, 2, rows, TILE)
            weighted = h_buf[...].reshape(chunk, units)
            tile = dot(weighted, w_down[:, at]).astype(BF16)
            o_buf[:, :, :, at] = tile.reshape(2, 2, rows, TILE)

        for copy in stores(step):
            copy.start()

    for action in after:
        action()
    for copy in stores(STEPS - 1):
        copy.wait()
    for copy in arrivals:
        copy.wait_recv()
    size = 32

    @pl.loop(0, rows // size)
    def _(i):
        at = pl.ds(pl.multiple_of(i * size, size), size)
        value = jobs[0].mine()[at].astype(F32)
        for j in range(3):
            value += landed[j, at].astype(F32)
        sum_out[at] = value

    dots_out[...] = dots_jobs[0].mine()[...] + dots_landed[0] + dots_landed[1] + dots_landed[2]
    line.finish()
    wire.close()


def feed_forward(x, few, g, mixed, shared, routed_down, shared_down, units):
    rows, width = x.shape
    copies = 3 + LINE_GATHER_COPIES + 5 * PLANE_GATHER_COPIES + 8 * PLANE_SCATTER_COPIES + 12
    return call(
        ffn_kernel,
        2,
        [
            ((LINE, PLANE, rows, width), BF16),
            ((rows, width), F32),
            (few.shape, F32),
            ((4, 2, LINE, rows, width), BF16),
            ((LINE, PLANE, rows, 2 * units), BF16),
            ((LINE, PLANE, rows, units), BF16),
        ],
        [x, few, g.reshape(LINE, PLANE, rows, width), mixed, shared, routed_down, shared_down],
        wires(copies)
        + [
            pltpu.SemaphoreType.DMA((14,)),
            pltpu.SemaphoreType.DMA((2,)),
            pltpu.SemaphoreType.DMA((3,)),
            pltpu.VMEM((2 * units, width), BF16),
            pltpu.VMEM((units, width), BF16),
            pltpu.VMEM((PLANE, LINE) + few.shape, F32),
            pltpu.VMEM((4, 4, 2, rows, width), BF16),
            pltpu.VMEM((3, rows, width), BF16),
            pltpu.VMEM((4, 4, 2) + few.shape, F32),
            pltpu.VMEM((3,) + few.shape, F32),
            pltpu.VMEM((4, rows, width), BF16),
            pltpu.VMEM((4, rows, width), BF16),
            pltpu.VMEM((2, 2, rows, width), BF16),
            pltpu.VMEM((4, rows, 2 * units), BF16),
            pltpu.VMEM((4, rows, units), BF16),
            pltpu.VMEM((4 * rows, 2 * units), F32),
            pltpu.VMEM((4 * rows, units), F32),
            pltpu.VMEM((4 * rows, LANES), F32),
            pltpu.VMEM((4 * rows, LANES), F32),
        ]
        + scatter_room(rows, width, BF16) * 4
        + scatter_room(few.shape[0], LANES, F32) * 4,
        out_specs=[HBM, VMEM, VMEM, HBM, HBM, HBM],
        in_specs=[VMEM, VMEM] + [HBM] * 5,
    )


def fan_kernel(block, after, out, send, recv, local):
    here, wire = Place(), Wire(send, recv)
    greet([here.plane(c) for c in (here.twin, here.across, here.along)])
    half = block.shape[0] // 2
    mine = pltpu.make_async_copy(block, out.at[here.c], local.at[0])
    mine.start()
    jobs = []
    for i in range(2):
        at = pl.ds(i * half, half)
        jobs.append(
            PlaneGather(
                wire, here, functools.partial(lambda at, c: out.at[c, at], at), block.at[at]
            ).first()
        )
    for job in jobs:
        job.second()
    for job in jobs:
        job.third()
    for job in jobs:
        job.finish()
    mine.wait()
    wire.close()


def fan_plane(block, after):
    return call(
        fan_kernel,
        5,
        [((PLANE,) + block.shape, block.dtype)],
        [block, after],
        wires(2 * PLANE_GATHER_COPIES) + [pltpu.SemaphoreType.DMA((1,))],
        in_specs=[VMEM, HBM],
    )[0].reshape(PLANE * block.shape[0], block.shape[1])


def end_kernel(
    parts, three, output, shared, bias, terms,
    out, three_out, output_out, shared_mid, shared_out, bias_out, terms_out,
    send, recv, local, held, three_held, output_held, *rooms
):
    here, wire = Place(), Wire(send, recv)
    room, three_room, output_room = rooms[:5], rooms[5:7], rooms[7:9]
    terms_in, terms_own, terms_line = rooms[9:]
    others = [(here.c + step) % PLANE for step in range(1, PLANE)]
    greet([here.plane(c) for c in others] + [here.line(z) for z in here.on_line()])
    on_line = here.on_line()
    loads = [
        pltpu.make_async_copy(three.at[:, z], three_held.at[z], local.at[z]) for z in range(LINE)
    ]
    loads += [
        pltpu.make_async_copy(parts, held, local.at[4]),
        pltpu.make_async_copy(output, output_held, local.at[5]),
        pltpu.make_async_copy(terms.at[here.c], terms_own, local.at[6]),
        pltpu.make_async_copy(bias, bias_out.at[here.z], local.at[7]),
    ]
    shared_own = pltpu.make_async_copy(shared.at[:, here.z], shared_mid.at[here.z], local.at[8])
    for copy in loads + [shared_own]:
        copy.start()
    job = PlaneScatter(wire, here, held, room)
    three_line = LineScatter(
        wire, here, [three_held.at[here.mirrored(i)] for i in range(4)], three_room
    )
    output_line = LineScatter(
        wire, here, [output_held.at[here.mirrored(i)] for i in range(4)], output_room
    )
    for copy in loads[:4]:
        copy.wait()
    three_line.begin()
    loads[4].wait()
    job.begin()
    shared_line = [
        wire.push(shared.at[:, z], shared_mid.at[here.z], here.line(z)) for z in on_line
    ]
    for copy in loads[5:]:
        copy.wait()
    output_line.begin()
    terms_plane = [
        wire.push(terms.at[c], terms_in.at[j], here.plane(c)) for j, c in enumerate(others)
    ]
    bias_line = [wire.push(bias, bias_out.at[here.z], here.line(z)) for z in on_line]
    job.first()
    job.second()
    job.third()
    out[...] = job.mine()[...].astype(F32)
    for copy in terms_plane:
        copy.wait_recv()
    total = terms_own[...]
    for j in range(PLANE - 1):
        total += terms_in[j]
    terms_own[...] = total
    terms_last = [
        wire.push(terms_own.at[z], terms_line.at[j], here.line(z)) for j, z in enumerate(on_line)
    ]
    three_line.first()
    output_line.first()
    three_line.second()
    shared_own.wait()
    for copy in shared_line:
        copy.wait_recv()
    shared_kept = pltpu.make_async_copy(shared_mid.at[:, here.c], shared_out.at[here.c], local.at[8])
    shared_kept.start()
    shared_plane = [
        wire.push(shared_mid.at[:, c], shared_out.at[here.c], here.plane(c)) for c in others
    ]
    output_line.second()
    three_line.third()
    three_plane = [
        wire.push(three_held.at[here.z, c], three_out.at[here.c], here.plane(c)) for c in others
    ]
    kept = pltpu.make_async_copy(three_held.at[here.z, here.c], three_out.at[here.c], local.at[0])
    kept.start()
    output_line.third()
    output_out[...] = output_held[here.z].astype(F32)
    for copy in terms_last:
        copy.wait_recv()
    terms_out[...] = terms_own[here.z] + terms_line[0] + terms_line[1] + terms_line[2]
    for copy in bias_line + shared_plane + three_plane:
        copy.wait_recv()
    kept.wait()
    shared_kept.wait()
    wire.close()


def line_room(shape, kind):
    return [pltpu.VMEM((3,) + shape, kind), pltpu.VMEM((2,) + shape, kind)]


def end_transfers(parts, three, output, shared, bias, terms):
    rows, width = parts.shape[0] // PLANE, parts.shape[1]
    _, _, owned, wide = three.shape
    copies = PLANE_SCATTER_COPIES + 2 * LINE_SCATTER_COPIES + 3 + 7 + 3 + 3 + 7 + 7
    out = call(
        end_kernel,
        6,
        [
            ((rows, width), F32),
            ((PLANE, owned, wide), BF16),
            ((owned, width), F32),
            ((LINE, PLANE) + shared.shape[2:], BF16),
            ((PLANE, LINE) + shared.shape[2:], BF16),
            ((LINE,) + bias.shape, F32),
            (terms.shape[2:], F32),
        ],
        [parts.reshape(4, 2, rows, width), three, output, shared, bias, terms],
        wires(copies)
        + [
            pltpu.SemaphoreType.DMA((9,)),
            pltpu.VMEM((4, 2, rows, width), BF16),
            pltpu.VMEM((LINE, PLANE, owned, wide), BF16),
            pltpu.VMEM((LINE, owned, width), BF16),
        ]
        + scatter_room(rows, width, BF16)
        + line_room((PLANE, owned, wide), BF16)
        + line_room((owned, width), BF16)
        + [
            pltpu.VMEM((PLANE - 1,) + terms.shape[1:], F32),
            pltpu.VMEM(terms.shape[1:], F32),
            pltpu.VMEM((3,) + terms.shape[2:], F32),
        ],
        out_specs=[VMEM, HBM, VMEM, HBM, HBM, HBM, VMEM],
        in_specs=[HBM] * 4 + [VMEM, HBM],
    )
    return out[:3] + out[4:]


def rms_scale(values):
    return lax.rsqrt(jnp.mean(values * values, axis=-1, keepdims=True) + EPS)


def rope_tables(places, head_size):
    half = head_size // 2
    freqs = jnp.exp(jnp.arange(half, dtype=F32) * (-2.0 * math.log(ROPE_BASE) / head_size))
    angles = places.astype(F32)[:, None] * freqs[None, :]
    return (jnp.cos(angles)[:, None, :], jnp.sin(angles)[:, None, :])


def rotate(values, cosine, sine):
    half = values.shape[-1] // 2
    first = values[..., :half]
    second = values[..., half:]
    return jnp.concatenate(
        [first * cosine - second * sine, second * cosine + first * sine], axis=-1
    )


def dot(left, right):
    return jnp.dot(left, right, preferred_element_type=F32)


def times_back(left, right):
    return lax.dot_general(left, right, (((1,), (1,)), ((), ())), preferred_element_type=F32)


def outer_sum(left, right):
    return lax.dot_general(left, right, (((0,), (0,)), ((), ())), preferred_element_type=F32)


def gather_plane(shard):
    return lax.all_gather(shard, "ctx", axis=0, tiled=True)


def scatter_plane(partial):
    return lax.psum_scatter(partial, "ctx", scatter_dimension=0, tiled=True)


def scatter_line(partial):
    return lax.psum_scatter(partial, "fsdp", scatter_dimension=0, tiled=False)


def over(step, carry, items, unrolled):
    if not unrolled:
        return lax.scan(step, carry, items)
    outs = []
    for i in range(jax.tree.leaves(items)[0].shape[0]):
        carry, out = step(carry, jax.tree.map(lambda item: item[i], items))
        outs.append(out)
    return carry, jax.tree.map(lambda *parts: jnp.stack(parts), *outs)


def blocks(length):
    return length // min(length, BLOCK)


def cut(array, axis=0):
    shape = array.shape
    count = blocks(shape[axis])
    shape = shape[:axis] + (count, shape[axis] // count) + shape[axis + 1 :]
    return jnp.moveaxis(array.reshape(shape), axis, 0)


def attend(queries, keys, values, starts):
    length = queries.shape[0]
    scale = 1.0 / math.sqrt(HEAD)
    cols = jnp.arange(length, dtype=jnp.int32)[None, :]

    def step(carry, items):
        part, low, rows = items
        mask = ((cols <= rows[:, None]) & (cols >= low[:, None]))[None]
        scores = jnp.einsum("qhd,khd->hqk", part, keys, preferred_element_type=F32)
        scores = jnp.where(mask, scores * scale, MASKED)
        best = jnp.max(scores, axis=-1, keepdims=True)
        weights = jnp.exp(scores - best)
        total = jnp.sum(weights, axis=-1, keepdims=True)
        probs = (weights / total).astype(BF16)
        out = jnp.einsum("hqk,khd->qhd", probs, values, preferred_element_type=F32)
        return carry, (out, best + jnp.log(total))

    items = (cut(queries), cut(starts), cut(cols[0]))
    _, (outs, logs) = over(step, 0, items, blocks(length) == 1)
    return outs.reshape(queries.shape), jnp.moveaxis(logs, 0, 1).reshape(-1, length, 1)


def attend_back(queries, keys, values, starts, logs, grad_attn, delta):
    length = queries.shape[0]
    scale = 1.0 / math.sqrt(HEAD)
    cols = jnp.arange(length, dtype=jnp.int32)[None, :]

    def step(carry, items):
        grad_keys, grad_values = carry
        part, low, rows, log, grad, less = items
        mask = ((cols <= rows[:, None]) & (cols >= low[:, None]))[None]
        scores = jnp.einsum("qhd,khd->hqk", part, keys, preferred_element_type=F32)
        probs = jnp.where(mask, jnp.exp(scores * scale - log), 0.0)
        grad_probs = jnp.einsum("qhd,khd->hqk", grad, values, preferred_element_type=F32)
        grad_scores = (probs * (grad_probs - less[:, :, None])).astype(BF16)
        grad_queries = scale * jnp.einsum(
            "hqk,khd->qhd", grad_scores, keys, preferred_element_type=F32
        )
        grad_keys += scale * jnp.einsum(
            "hqk,qhd->khd", grad_scores, part, preferred_element_type=F32
        )
        grad_values += jnp.einsum(
            "hqk,qhd->khd", probs.astype(BF16), grad, preferred_element_type=F32
        )
        return (grad_keys, grad_values), grad_queries

    zeros = jnp.zeros(keys.shape, F32)
    items = (cut(queries), cut(starts), cut(cols[0]), cut(logs, 1), cut(grad_attn), cut(delta, 1))
    carry, grad_queries = over(step, (zeros, zeros), items, blocks(length) == 1)
    return grad_queries.reshape(queries.shape), carry[0], carry[1]


def body(
    tokens,
    positions,
    routes,
    cotangent,
    attn_gain,
    query_weight,
    key_weight,
    value_weight,
    query_bias,
    key_bias,
    value_bias,
    output_weight,
    ffn_gain,
    router_weight,
    expert_gate,
    expert_up,
    expert_down,
    shared_gate,
    shared_up,
    shared_down,
    shared_sigmoid,
):
    plane, line = lax.axis_size("ctx"), lax.axis_size("fsdp")
    place = lax.axis_index("ctx")
    rows, width = tokens.shape[1], tokens.shape[2]
    length = plane * rows
    experts = router_weight.shape[1]
    groups = math.gcd(HEADS, plane)
    share = plane // groups
    heads = HEADS // groups
    span = heads * HEAD
    owned = width // (plane * line)
    group = place // share

    fast = (plane, line) == (PLANE, LINE) and share == 1
    three = jnp.stack([query_weight, key_weight, value_weight])
    routed_units, shared_units = expert_down.shape[1], shared_down.shape[0]
    columns = [attn_gain, query_bias, key_bias, value_bias, ffn_gain, shared_sigmoid]
    columns = jnp.concatenate([jnp.stack(columns, axis=1), router_weight], axis=1)
    x_own, g_own = tokens[0], cotangent[0]
    shared = [w.reshape(owned, plane * line, shared_units) for w in (shared_gate, shared_up)]
    shared = jnp.concatenate(shared, axis=2).transpose(1, 0, 2)
    routed = jnp.stack([expert_gate[0].T, expert_up[0].T]).reshape(2, line, routed_units, -1)
    routed = routed.transpose(1, 0, 2, 3)
    if fast:
        high, low = positions[0] // 64, positions[0] % 64
        digits = jnp.stack([high, low]).reshape(2 * (rows // owned), owned).T.astype(BF16)
        small = jnp.concatenate([columns, digits], axis=1)
        marks = small.shape[1]
        small = jnp.pad(small, ((0, 0), (0, LANES - marks)))
        sent = three.reshape(3, owned, plane, span).transpose(2, 1, 0, 3)
        x_all, w_three, w_output, small, shared, g_sent = start_transfers(
            x_own,
            sent.reshape(plane, owned, 3 * span),
            output_weight,
            small,
            shared.reshape(plane, line, owned, 2 * shared_units),
            g_own,
        )
        routed = routed.reshape(line, 2 * routed_units, -1)
        routed = lax.all_to_all(routed, "fsdp", split_axis=0, concat_axis=0, tiled=True)
        x_all = x_all.reshape(length, width)
        w_three = w_three.reshape(width, 3 * span)
        w_output = w_output.reshape(span, width)
        digits = lax.dynamic_index_in_dim(small, lax.axis_index("fsdp"), 1, keepdims=False)
        digits = digits[:, :, columns.shape[1] : marks].astype(jnp.int32)
        digits = digits.transpose(0, 2, 1).reshape(plane, 2, rows)
        places = (digits[:, 0] * 64 + digits[:, 1]).reshape(length)
        small = small.reshape(width, LANES)[:, : columns.shape[1]]
        g_all = lax.all_gather(g_sent, ("fsdp", "ctx"), axis=0, tiled=True)
    else:
        small = lax.all_gather(columns, BOTH, axis=0, tiled=True)
        places = lax.all_gather(positions[0], "ctx", axis=0, tiled=True)
        x_all = gather_plane(x_own)
        whole = lax.all_gather(three, BOTH, axis=1, tiled=True)
        whole = lax.dynamic_slice_in_dim(whole, group * span, span, 2)
        w_three = whole.transpose(1, 0, 2).reshape(width, 3 * span)
        w_output = lax.all_gather(output_weight, BOTH, axis=0, tiled=True)
        w_output = lax.dynamic_slice_in_dim(w_output, group * span, span, 0)
    gain_in = small[:, 0].astype(F32)
    gain_mid = small[:, 4].astype(F32)
    w_switch = small[:, 5]
    w_router = small[:, 6:]
    biases = lax.dynamic_slice_in_dim(small[:, 1:4], group * span, span, 0).astype(F32)
    biases = biases.T.reshape(3 * span)
    used = routed_units + shared_units
    units = -(-used // LANES) * LANES

    states = x_all.astype(F32)
    starts = jnp.arange(length, dtype=jnp.int32) - places
    unit_in = states * rms_scale(states)
    normed = (unit_in * gain_in[None, :]).astype(BF16)
    cosine, sine = rope_tables(places, HEAD)
    pre = (dot(normed, w_three) + biases[None, :]).reshape(length, 3, heads, HEAD)
    queries = rotate(pre[:, 0], cosine, sine).astype(BF16)
    keys = rotate(pre[:, 1], cosine, sine).astype(BF16)
    values = pre[:, 2].astype(BF16)
    attn_rows, logs = attend(queries, keys, values, starts)
    if share > 1:
        mine = jnp.arange(length, dtype=jnp.int32) // (length // share) == place % share
        attn_rows = jnp.where(mine[:, None, None], attn_rows, 0.0)
    attn_low = attn_rows.reshape(length, span).astype(BF16)
    branch = dot(attn_low, w_output).astype(BF16)
    if fast:
        branch, shared = fold_plane(branch, shared)
    else:
        branch = scatter_plane(branch).astype(F32)
    mid = x_own.astype(F32) + branch

    scale_mid = rms_scale(mid)
    unit_mid = mid * scale_mid
    normed2 = (unit_mid * gain_mid[None, :]).astype(BF16)
    router_probs = jax.nn.softmax(dot(normed2, w_router), axis=-1)
    picks = routes[0][:, :, None] == jnp.arange(experts, dtype=jnp.int32)[None, None, :]
    hits = jnp.any(picks, axis=1)
    switch = jax.nn.sigmoid(dot(normed2, w_switch[:, None]))
    factors = jnp.concatenate([jnp.where(hits, router_probs, 0.0), switch], axis=1)
    mine = jnp.arange(experts, dtype=jnp.int32) == place

    def hidden_units(x_all, g_all, by_route, by_switch, w_both, w_down):
        number = jnp.arange(units, dtype=jnp.int32)
        by = jnp.where(number < routed_units, by_route[:, None], by_switch[:, None])
        pre = times_back(x_all, w_both)
        gate_pre, up_pre = pre[:, :units], pre[:, units:]
        grad_hidden = times_back(g_all, w_down)
        sigma = jax.nn.sigmoid(gate_pre)
        act = gate_pre * sigma
        hidden = act * up_pre
        product = hidden * grad_hidden
        routed_dot = jnp.sum(product[:, :routed_units], axis=1)
        shared_dot = jnp.sum(product[:, routed_units:used], axis=1)
        weighted = (hidden * by).astype(BF16)
        slope = sigma * (1.0 + gate_pre * (1.0 - sigma))
        grad_hidden = grad_hidden * by
        grad_pre = jnp.concatenate([grad_hidden * up_pre * slope, grad_hidden * act], axis=1)
        grad_pre = grad_pre.astype(BF16)
        grad_part = dot(grad_pre, w_both).astype(BF16)
        out_part = dot(weighted, w_down).astype(BF16)
        terms = (outer_sum(grad_pre, x_all), outer_sum(weighted, g_all))
        return terms, out_part, grad_part, routed_dot, shared_dot

    def units_of(routed, shared, spare):
        return jnp.concatenate([routed[0], shared[0], spare, routed[1], shared[1], spare], axis=0)

    def parts_of(term):
        routed = [term[:routed_units], term[units : units + routed_units]]
        shared = [term[routed_units:used], term[units + routed_units : units + used]]
        return jnp.stack(routed), jnp.stack(shared)

    if fast:
        few = jnp.pad(factors.T, ((0, 16 - experts - 1), (0, 0)))
        shared = shared.reshape(width, 2 * shared_units).T
        x_all, grad_ffn, dots, out_part, grad_pre, weighted = feed_forward(
            normed2, few, g_all, routed, shared, expert_down[0], shared_down, units
        )
        ffn = scatter_plane(out_part.reshape(plane * line * rows, width))
        ffn = scatter_line(ffn.reshape(line, rows, width)).astype(F32)
        term_both = outer_sum(
            grad_pre.reshape(line * length, 2 * units), x_all.reshape(line * length, width)
        )
        term_down = outer_sum(weighted.reshape(line * length, units), g_all)
        routed, shared = parts_of(term_both.astype(BF16))
        routed = routed.reshape(2 * routed_units, line, -1).transpose(1, 0, 2)
        routed_sent = routed
        routed = lax.all_to_all(routed, "fsdp", split_axis=0, concat_axis=0, tiled=True)
        routed = routed.reshape(line, 2, routed_units, -1)
        shared = shared.reshape(2 * shared_units, width).T
        shared = shared.reshape(plane, line, owned, 2 * shared_units)
        dots = dots[: experts + 1].T
    else:
        routed = lax.all_to_all(routed, "fsdp", split_axis=0, concat_axis=0, tiled=True)
        routed = routed.transpose(1, 2, 0, 3).reshape(2, routed_units, width)
        spare = jnp.zeros((units - used, width), BF16)
        w_down = jnp.concatenate([expert_down[0], shared_down, spare], axis=0)
        factors = lax.all_gather(factors, ("fsdp", "ctx"), axis=0, tiled=True)
        factors = factors.reshape(line, length, experts + 1)
        x_line = lax.all_gather(normed2, "fsdp", axis=0, tiled=False)
        g_line = lax.all_gather(g_own, "fsdp", axis=0, tiled=False)

        shared = lax.all_to_all(shared, BOTH, split_axis=0, concat_axis=0, tiled=True)
        shared = shared.reshape(width, 2, shared_units).transpose(1, 2, 0)
        w_both = units_of(routed, shared, spare)

        def step(terms, items):
            x_part, g_part, factor = items
            by_route = jnp.sum(jnp.where(mine, factor[:, :experts], 0.0), axis=1)
            more, out_part, grad_part, routed_dot, shared_dot = hidden_units(
                gather_plane(x_part), gather_plane(g_part), by_route, factor[:, experts], w_both, w_down
            )
            dots = jnp.where(mine, routed_dot[:, None], 0.0)
            dots = jnp.concatenate([dots, shared_dot[:, None]], axis=1)
            terms = tuple(term + part for term, part in zip(terms, more))
            return terms, (scatter_plane(out_part), scatter_plane(grad_part), dots)

        terms = tuple(jnp.zeros(w.shape, F32) for w in (w_both, w_down))
        terms, (out_parts, grad_parts, dots) = lax.scan(step, terms, (x_line, g_line, factors))
        term_both, term_down = terms
        grad_ffn = scatter_line(grad_parts).astype(F32)
        ffn = scatter_line(out_parts).astype(F32)
        dots = dots.reshape(line, plane, rows, experts + 1)
        dots = lax.psum_scatter(dots, "ctx", scatter_dimension=1, tiled=False)
        dots = scatter_line(dots)

        routed, shared = parts_of(term_both.astype(BF16))
        grad_shared_gate, grad_shared_up = [
            lax.all_to_all(t.T, BOTH, split_axis=0, concat_axis=1, tiled=True).astype(F32)
            for t in shared
        ]
        routed = routed.reshape(2, routed_units, line, -1).transpose(2, 0, 1, 3)
        routed = lax.all_to_all(routed, "fsdp", split_axis=0, concat_axis=0, tiled=True)
    grad_expert_down = term_down[:routed_units][None]
    grad_shared_down = term_down[routed_units:used]

    grad_out = cotangent[0].astype(F32)
    grad_probs = jnp.where(hits, dots[:, :experts], 0.0)
    grad_logits = (
        router_probs * (grad_probs - jnp.sum(router_probs * grad_probs, axis=-1, keepdims=True))
    ).astype(BF16)
    grad_switch = dots[:, experts:] * switch * (1.0 - switch)
    grad_normed2 = (
        grad_ffn + times_back(grad_logits, w_router) + grad_switch * w_switch.astype(F32)[None, :]
    )
    scaled_mid = grad_normed2 * gain_mid[None, :]
    grad_mid = grad_out + scale_mid * (
        scaled_mid - unit_mid * jnp.mean(scaled_mid * unit_mid, axis=-1, keepdims=True)
    )
    terms = jnp.concatenate(
        [
            jnp.sum(grad_normed2 * unit_mid, axis=0)[:, None],
            jnp.sum(grad_switch * normed2.astype(F32), axis=0)[:, None],
            outer_sum(normed2, grad_logits),
        ],
        axis=1,
    )

    grad_branch = grad_mid.astype(BF16)
    if fast:
        grad_branch = fan_plane(grad_branch, routed_sent)
    else:
        grad_branch = gather_plane(grad_branch)
    routed = routed.transpose(1, 3, 0, 2).reshape(2, 1, -1, line * routed_units).astype(F32)
    grad_attn = times_back(grad_branch, w_output).reshape(length, heads, HEAD).astype(BF16)
    if share > 1:
        mine = jnp.arange(length, dtype=jnp.int32) // (length // share) == place % share
        grad_attn = jnp.where(mine[:, None, None], grad_attn, 0)
    delta = jnp.sum(grad_attn.astype(F32) * attn_rows, axis=-1).T
    grad_queries, grad_keys, grad_values = attend_back(
        queries, keys, values, starts, logs, grad_attn, delta
    )
    grad_pre = jnp.concatenate(
        [
            rotate(grad_queries, cosine, -sine).reshape(length, span),
            rotate(grad_keys, cosine, -sine).reshape(length, span),
            grad_values.reshape(length, span),
        ],
        axis=1,
    ).astype(BF16)
    grad_part = times_back(grad_pre, w_three).astype(BF16)
    term_three = outer_sum(normed, grad_pre)
    term_output = outer_sum(attn_low, grad_branch)
    term_bias = jnp.sum(grad_pre.astype(F32), axis=0)
    if fast:
        count = terms.shape[1]
        terms = terms.reshape(plane, line, owned * count)
        terms = jnp.pad(terms, ((0, 0), (0, 0), (0, 8 * LANES - owned * count)))
        grad_normed, grad_three, grad_output, shared, term_bias, terms = end_transfers(
            grad_part,
            term_three.astype(BF16).reshape(plane, line, owned, 3 * span),
            term_output.astype(BF16).reshape(line, owned, width),
            shared,
            jnp.broadcast_to(term_bias[None], (8, 3 * span)),
            terms.reshape(plane, line, 8, LANES),
        )
        grad_three = grad_three.reshape(plane, owned, 3, span).transpose(2, 1, 0, 3)
        grad_three = grad_three.reshape(3, owned, width).astype(F32)
        term_bias = jnp.sum(term_bias[:, 0], axis=0).reshape(3, line, owned)
        grad_bias = lax.dynamic_index_in_dim(term_bias, lax.axis_index("fsdp"), 1, keepdims=False)
        terms = terms.reshape(-1)[: owned * count].reshape(owned, count)
        shared = shared.reshape(plane * line, owned, 2, shared_units).transpose(2, 1, 0, 3)
        shared = shared.reshape(2, owned, -1).astype(F32)
        grad_shared_gate, grad_shared_up = shared[0], shared[1]
    else:
        grad_normed = scatter_plane(grad_part).astype(F32)
        zeros = jnp.zeros((3, width, width), BF16)
        spread = lax.dynamic_update_slice_in_dim(
            zeros, term_three.astype(BF16).reshape(width, 3, span).transpose(1, 0, 2), group * span, 2
        )
        grad_three = lax.psum_scatter(spread, BOTH, scatter_dimension=1, tiled=True).astype(F32)
        spread = lax.dynamic_update_slice_in_dim(
            zeros[0], term_output.astype(BF16), group * span, 0
        )
        grad_output = lax.psum_scatter(spread, BOTH, scatter_dimension=0, tiled=True).astype(F32)
        spread = lax.dynamic_update_slice_in_dim(
            jnp.zeros((3, width), F32), term_bias.reshape(3, span), group * span, 1
        )
        grad_bias = lax.psum_scatter(spread, BOTH, scatter_dimension=1, tiled=True)
        terms = lax.psum_scatter(terms, BOTH, scatter_dimension=0, tiled=True)
    grad_attn_gain = jnp.sum(three.astype(F32) * grad_three, axis=(0, 2)) / attn_gain.astype(F32)
    own_states = tokens[0].astype(F32)
    scale_in = rms_scale(own_states)
    own_unit = own_states * scale_in
    scaled_in = grad_normed * gain_in[None, :]
    grad_states = grad_mid + scale_in * (
        scaled_in - own_unit * jnp.mean(scaled_in * own_unit, axis=-1, keepdims=True)
    )
    return (
        (mid + ffn).astype(BF16)[None],
        grad_states[None],
        grad_attn_gain,
        grad_three[0],
        grad_three[1],
        grad_three[2],
        grad_bias[0],
        grad_bias[1],
        grad_bias[2],
        grad_output,
        terms[:, 0],
        terms[:, 2:],
        routed[0],
        routed[1],
        grad_expert_down,
        grad_shared_gate,
        grad_shared_up,
        grad_shared_down,
        terms[:, 1],
    )


def solution(mesh):
    tokens, flat, both, routed = (
        P("fsdp", "ctx", None),
        P(BOTH),
        P(BOTH, None),
        P("ctx", "fsdp", None),
    )
    weights = (flat, both, both, both, flat, flat, flat, both, flat, both)
    weights += (routed, routed, routed, both, both, both, flat)
    return jax.shard_map(
        body,
        mesh=mesh,
        in_specs=(tokens, P("fsdp", "ctx"), tokens, tokens) + weights,
        out_specs=(tokens, tokens) + weights,
        check_vma=False,
    )
```

```python
import functools
import math

import jax
import jax.numpy as jnp
from jax import lax
from jax.experimental import pallas as pl
from jax.experimental.pallas import tpu as pltpu
from jax.sharding import PartitionSpec as P

HEADS = 16
HEAD = 128
EPS = 1e-06
ROPE_BASE = 1000000.0
MASKED = -1e30
BLOCK = 1024
BOTH = ("ctx", "fsdp")
BF16 = jnp.bfloat16
F32 = jnp.float32


PLANE, LINE = 8, 4
LANES = 128
HBM = pl.BlockSpec(memory_space=pl.ANY)
VMEM = pl.BlockSpec(memory_space=pltpu.VMEM)


class Place:
    def __init__(self):
        self.c = lax.axis_index("ctx")
        self.z = lax.axis_index("fsdp")
        self.core = self.c % 2
        self.x = (self.c // 2) % 2
        self.y = self.c // 4
        self.twin = self.c + 1 - 2 * self.core
        self.across = self.c + 2 - 4 * self.x
        self.along = self.c + 4 - 8 * self.y
        self.far = self.across + 4 - 8 * self.y
        self.upper = self.z // 2
        self.depth = self.z + self.upper * (3 - 2 * self.z)
        self.near = self.z + 1 - 2 * (self.z % 2)
        self.middle = 3 - self.z

    def mirrored(self, number):
        return number + self.upper * (3 - 2 * number)

    def plane(self, c):
        return (c, self.z)

    def line(self, z):
        return (self.c, z)

    def on_line(self):
        return [(self.z + step) % LINE for step in (2, 1, 3)]


class Wire:
    def __init__(self, send, recv):
        self.send, self.recv, self.used, self.open = send, recv, 0, []

    def copy(self, source, target, device, arrival=None):
        number = self.used
        self.used += 1
        return pltpu.make_async_remote_copy(
            src_ref=source,
            dst_ref=target,
            send_sem=self.send.at[number],
            recv_sem=self.recv.at[number if arrival is None else arrival],
            device_id=device,
            device_id_type=pl.DeviceIdType.MESH,
        )

    def later(self, source, target, device, arrival=None):
        copy = self.copy(source, target, device, arrival)
        self.open.append(copy)
        return copy

    def push(self, source, target, device):
        copy = self.later(source, target, device)
        copy.start()
        return copy

    def close(self):
        for copy in self.open:
            copy.wait_send()


def greet(devices):
    barrier = pltpu.get_barrier_semaphore()
    for device in devices:
        pl.semaphore_signal(
            barrier, inc=1, device_id=device, device_id_type=pl.DeviceIdType.MESH
        )
    pl.semaphore_wait(barrier, len(devices))


class PlaneGather:
    def __init__(self, wire, here, at, source=None):
        source = at(here.c) if source is None else source
        to_x, to_y = here.plane(here.across), here.plane(here.along)
        to_twin = here.plane(here.twin)
        x_block, y_block, far_block = at(here.across), at(here.along), at(here.far)
        half = x_block.shape[0] // 2
        high, low = x_block.at[pl.ds(half, half)], y_block.at[pl.ds(0, half)]
        self.from_x = wire.later(source, at(here.c), to_x)
        self.from_y = wire.later(source, at(here.c), to_y)
        self.far_y = wire.later(high, high, to_y)
        self.far_x = wire.later(low, low, to_x)
        blocks = [(source, at(here.c))] + [(b, b) for b in (x_block, y_block, far_block)]
        self.twins = [wire.later(block, target, to_twin) for block, target in blocks]

    def first(self):
        self.from_x.start()
        self.from_y.start()
        self.twins[0].start()
        return self

    def second(self):
        self.from_x.wait_recv()
        self.far_y.start()
        self.twins[1].start()
        self.from_y.wait_recv()
        self.far_x.start()
        self.twins[2].start()

    def third(self):
        self.far_x.wait_recv()
        self.far_y.wait_recv()
        self.twins[3].start()

    def finish(self):
        for copy in self.twins:
            copy.wait_recv()


PLANE_GATHER_COPIES = 8


class LineGather:
    def __init__(self, wire, here, at, source=None):
        self.wire, self.here, self.at = wire, here, at
        source = at(here.z) if source is None else source
        self.one = wire.push(source, at(here.z), here.line(here.near))
        inner = here.depth == 1
        middle, near = here.line(here.middle), here.line(here.near)
        own, mine = source, at(here.z)
        end, two, three = at(here.mirrored(0)), at(here.mirrored(2)), at(here.mirrored(3))
        self.inner = inner
        self.two_in = wire.copy(own, mine, middle)
        self.three_in = wire.copy(end, end, middle)
        self.two_out = wire.copy(two, two, near)
        self.three_out = wire.copy(three, three, near)

        @pl.when(inner)
        def _():
            self.two_in.start()

    def first(self):
        self.one.wait_recv()
        pl.when(self.inner)(self.three_in.start)

    def second(self):
        @pl.when(self.inner)
        def _():
            self.two_in.wait_recv()
            self.two_out.start()

        @pl.when(self.here.depth == 0)
        def _():
            self.two_out.wait_recv()

    def third(self):
        @pl.when(self.inner)
        def _():
            self.three_in.wait_recv()
            self.three_out.start()

        @pl.when(self.here.depth == 0)
        def _():
            self.three_out.wait_recv()

    def order(self):
        here = self.here
        return [here.z, here.near, here.mirrored(2), here.mirrored(3)]

    def finish(self):
        @pl.when(self.inner)
        def _():
            for copy in (self.two_in, self.three_in, self.two_out, self.three_out):
                copy.wait_send()


LINE_GATHER_COPIES = 5


def add_into(total, part):
    rows = total.shape[0]
    step = min(rows, 32)

    @pl.loop(0, rows // step)
    def _(i):
        at = pl.ds(pl.multiple_of(i * step, step), step)
        total[at] = total[at] + part[at]


class PlaneScatter:
    def __init__(self, wire, here, parts, room):
        self.here, self.parts, self.room = here, parts, room
        arrived, one_x, one_y, two_x, two_y = room
        self.half = arrived.shape[1] // 2
        to_x, to_y = here.plane(here.across), here.plane(here.along)
        self.twin = wire.later(parts.at[:, 1 - here.core], arrived, here.plane(here.twin))
        self.from_x = [
            wire.later(self.block(y, 1 - here.x, 0), one_x.at[y], to_x) for y in range(2)
        ]
        self.from_y = [
            wire.later(self.block(1 - here.y, x, 1), one_y.at[x], to_y) for x in range(2)
        ]
        self.last_y = wire.later(self.block(1 - here.y, here.x, 0), two_y, to_y)
        self.last_x = wire.later(self.block(here.y, 1 - here.x, 1), two_x, to_x)

    def block(self, y, x, half=None):
        if half is None:
            return self.parts.at[y * 2 + x, self.here.core]
        return self.parts.at[y * 2 + x, self.here.core, pl.ds(half * self.half, self.half)]

    def begin(self):
        self.twin.start()

    def first(self):
        self.twin.wait_recv()
        for i in range(4):
            add_into(self.parts.at[i, self.here.core], self.room[0].at[i])
        for copy in self.from_x + self.from_y:
            copy.start()

    def second(self):
        here, one_x, one_y = self.here, self.room[1], self.room[2]
        for copy in self.from_x:
            copy.wait_recv()
        add_into(self.block(1 - here.y, here.x, 0), one_x.at[1 - here.y])
        self.last_y.start()
        for copy in self.from_y:
            copy.wait_recv()
        add_into(self.block(here.y, 1 - here.x, 1), one_y.at[1 - here.x])
        self.last_x.start()
        add_into(self.block(here.y, here.x, 0), one_x.at[here.y])
        add_into(self.block(here.y, here.x, 1), one_y.at[here.x])

    def third(self):
        here, two_x, two_y = self.here, self.room[3], self.room[4]
        self.last_y.wait_recv()
        add_into(self.block(here.y, here.x, 0), two_y)
        self.last_x.wait_recv()
        add_into(self.block(here.y, here.x, 1), two_x)

    def mine(self):
        return self.block(self.here.y, self.here.x)


PLANE_SCATTER_COPIES = 7


class LineScatter:
    def __init__(self, wire, here, blocks, room):
        self.here, self.blocks = here, blocks
        near, middle = here.line(here.near), here.line(here.middle)
        self.ends, self.mids = room
        own = self.blocks
        self.out = [wire.copy(own[i], self.ends.at[k], near) for k, i in enumerate((2, 3, 1))]
        self.over = [wire.copy(own[i], self.mids.at[k], middle) for k, i in enumerate((2, 3))]
        self.home = wire.copy(own[0], self.ends.at[0], near)

    def begin(self):
        @pl.when(self.here.depth == 0)
        def _():
            for copy in self.out:
                copy.start()

    def first(self):
        @pl.when(self.here.depth == 1)
        def _():
            for k in range(2):
                self.out[k].wait_recv()
                add_into(self.blocks[2 + k], self.ends.at[k])
                self.over[k].start()

    def second(self):
        @pl.when(self.here.depth == 1)
        def _():
            self.over[1].wait_recv()
            add_into(self.blocks[0], self.mids.at[1])
            self.home.start()
            self.out[2].wait_recv()
            add_into(self.blocks[1], self.ends.at[2])
            self.over[0].wait_recv()
            add_into(self.blocks[1], self.mids.at[0])

    def third(self):
        @pl.when(self.here.depth == 0)
        def _():
            self.home.wait_recv()
            add_into(self.blocks[0], self.ends.at[0])
            for copy in self.out:
                copy.wait_send()

        @pl.when(self.here.depth == 1)
        def _():
            for copy in self.over + [self.home]:
                copy.wait_send()


LINE_SCATTER_COPIES = 6


def scatter_room(rows, columns, kind):
    half = rows // 2
    return [
        pltpu.VMEM((4, rows, columns), kind),
        pltpu.VMEM((2, half, columns), kind),
        pltpu.VMEM((2, half, columns), kind),
        pltpu.VMEM((half, columns), kind),
        pltpu.VMEM((half, columns), kind),
    ]


def wires(count):
    return [pltpu.SemaphoreType.DMA((count,)), pltpu.SemaphoreType.DMA((count,))]


def call(kernel, number, outs, args, scratch, out_specs=None, in_specs=None, aliases=None):
    return pl.pallas_call(
        kernel,
        out_shape=[jax.ShapeDtypeStruct(shape, kind) for shape, kind in outs],
        in_specs=in_specs or [HBM] * len(args),
        out_specs=out_specs or [HBM] * len(outs),
        scratch_shapes=scratch,
        input_output_aliases=aliases or {},
        compiler_params=pltpu.CompilerParams(
            collective_id=number, has_side_effects=True, vmem_limit_bytes=60 << 20
        ),
    )(*args)


def start_kernel(
    tokens, three, output, small, shared, x_out, three_out, output_out, small_out, shared_out,
    send, recv, local
):
    here, wire = Place(), Wire(send, recv)
    others = [(here.c + step) % PLANE for step in range(1, PLANE)]
    greet([here.plane(c) for c in others] + [here.line(z) for z in here.on_line()])
    small_line = [
        wire.push(small, small_out.at[here.c, here.z], here.line(z)) for z in here.on_line()
    ]
    plane = [
        wire.push(three.at[c], three_out.at[here.c, here.z], here.plane(c)) for c in others
    ]
    mine = [
        pltpu.make_async_copy(small, small_out.at[here.c, here.z], local.at[0]),
        pltpu.make_async_copy(three.at[here.c], three_out.at[here.c, here.z], local.at[1]),
        pltpu.make_async_copy(tokens, x_out.at[here.c], local.at[2]),
        pltpu.make_async_copy(output, output_out.at[here.z], local.at[3]),
        pltpu.make_async_copy(shared.at[:, here.z], shared_out.at[here.z], local.at[4]),
    ]
    for copy in mine:
        copy.start()
    x_plane = PlaneGather(wire, here, lambda c: x_out.at[c], tokens).first()
    for copy in mine:
        copy.wait()
    for copy in small_line + plane:
        copy.wait_recv()
    three_line = LineGather(wire, here, lambda z: three_out.at[:, z])
    output_line = LineGather(wire, here, lambda z: output_out.at[z])
    small_plane = PlaneGather(wire, here, lambda c: small_out.at[c]).first()
    moved = [
        wire.push(shared.at[:, z], shared_out.at[here.z], here.line(z)) for z in here.on_line()
    ]
    x_plane.second()
    small_plane.second()
    x_plane.third()
    small_plane.third()
    three_line.first()
    output_line.first()
    three_line.second()
    output_line.second()
    three_line.third()
    output_line.third()
    x_plane.finish()
    small_plane.finish()
    for copy in moved:
        copy.wait_recv()
    three_line.finish()
    output_line.finish()
    wire.close()


def start_transfers(tokens, three, output, small, shared):
    rows, width = tokens.shape
    _, owned, wide = three.shape
    copies = 3 + 7 + 3 + 2 * PLANE_GATHER_COPIES + 2 * LINE_GATHER_COPIES
    return call(
        start_kernel,
        1,
        [
            ((PLANE, rows, width), BF16),
            ((PLANE, LINE, owned, wide), BF16),
            ((LINE, owned, width), BF16),
            ((PLANE, LINE) + small.shape, BF16),
            ((LINE, PLANE) + shared.shape[2:], BF16),
        ],
        [tokens, three, output, small, shared],
        wires(copies) + [pltpu.SemaphoreType.DMA((5,))],
        in_specs=[VMEM] * 5,
    )


def fold_kernel(parts, shared, out, shared_out, *scratch):
    here, wire = Place(), Wire(scratch[0], scratch[1])
    local = scratch[2]
    others = [(here.c + step) % PLANE for step in range(1, PLANE)]
    greet([here.plane(c) for c in others])
    kept = pltpu.make_async_copy(shared.at[:, here.c], shared_out.at[here.c], local.at[2])
    kept.start()
    half = parts.shape[2] // 2
    jobs, loads = [], []
    for i in range(2):
        held, room = scratch[3 + 6 * i], scratch[4 + 6 * i : 9 + 6 * i]
        loads.append(
            pltpu.make_async_copy(parts.at[:, :, pl.ds(i * half, half)], held, local.at[i])
        )
        loads[i].start()
        jobs.append(PlaneScatter(wire, here, held, room))
    for load, job in zip(loads, jobs):
        load.wait()
        job.begin()
    moved = [wire.push(shared.at[:, c], shared_out.at[here.c], here.plane(c)) for c in others]
    for job in jobs:
        job.first()
    for job in jobs:
        job.second()
    for i, job in enumerate(jobs):
        job.third()
        out[pl.ds(i * half, half)] = job.mine()[...].astype(out.dtype)
    for copy in moved:
        copy.wait_recv()
    kept.wait()
    wire.close()


def held_room(rows, columns, kind):
    return [pltpu.VMEM((4, 2, rows, columns), kind)] + scatter_room(rows, columns, kind)


def fold_plane(parts, shared):
    rows, width = parts.shape[0] // PLANE, parts.shape[1]
    return call(
        fold_kernel,
        3,
        [((rows, width), F32), ((PLANE, LINE) + shared.shape[2:], BF16)],
        [parts.reshape(4, 2, rows, width), shared],
        wires(2 * PLANE_SCATTER_COPIES + 7)
        + [pltpu.SemaphoreType.DMA((3,))]
        + held_room(rows // 2, width, BF16) * 2,
        out_specs=[VMEM, HBM],
    )


STEPS, TILE = 8, 512


def ffn_kernel(
    x, few, g, mixed, shared, routed_down, shared_down, x_out, sum_out, dots_out, out_parts, pre_out, weighted_out,
    send, recv, local, fetch, store, w_both, w_down, few_all, parts, landed, dots_parts, dots_landed,
    x_buf, g_buf, o_buf, p_buf, h_buf, pre_buf, back_buf, by_buf, dot_buf, *rooms
):
    here, wire = Place(), Wire(send, recv)
    rows, width = x.shape
    chunk = 4 * rows
    routed, units = routed_down.shape[0], w_down.shape[0]
    used = routed + shared_down.shape[0]
    few_rows = few.shape[0]
    greet(
        [here.plane(c) for c in (here.twin, here.across, here.along)]
        + [here.line(z) for z in here.on_line()]
    )
    own = pltpu.make_async_copy(x, x_out.at[here.z, here.c], local.at[0])
    own.start()
    own_few = pltpu.make_async_copy(few, few_all.at[here.c, here.z], local.at[1])
    own_few.start()
    part = mixed.shape[2]
    pieces = [
        (mixed.at[z, pl.ds(k * routed, routed)], w_both.at[pl.ds(k * units, routed), pl.ds(z * part, part)])
        for z in range(LINE)
        for k in range(2)
    ]
    pieces += [
        (
            shared.at[pl.ds(k * (used - routed), used - routed)],
            w_both.at[pl.ds(k * units + routed, used - routed)],
        )
        for k in range(2)
    ]
    pieces += [
        (routed_down, w_down.at[pl.ds(0, routed)]),
        (shared_down, w_down.at[pl.ds(routed, used - routed)]),
    ]
    weights = [
        pltpu.make_async_copy(source, target, local.at[2 + i])
        for i, (source, target) in enumerate(pieces)
    ]
    for copy in weights:
        copy.start()
    nothing = jnp.zeros((units - used, width), BF16)
    w_both[pl.ds(used, units - used)] = nothing
    w_both[pl.ds(units + used, units - used)] = nothing
    w_down[pl.ds(used, units - used)] = nothing
    few_line = [
        wire.push(few, few_all.at[here.c, here.z], here.line(z)) for z in here.on_line()
    ]
    line = LineGather(wire, here, lambda z: x_out.at[z, here.c], x)
    order = line.order()
    planes = [
        PlaneGather(
            wire, here, functools.partial(lambda z, c: x_out.at[z, c], order[i]), None if i else x
        )
        for i in range(4)
    ]
    few_plane = PlaneGather(wire, here, lambda c: few_all.at[c])
    jobs = [PlaneScatter(wire, here, parts.at[i], rooms[5 * i : 5 * i + 5]) for i in range(4)]
    dots_jobs = [
        PlaneScatter(wire, here, dots_parts.at[i], rooms[20 + 5 * i : 25 + 5 * i])
        for i in range(4)
    ]
    slots = [None, 0, 1 + here.depth, 2 - here.depth]
    base = wire.used
    arrivals = [
        wire.copy(source.at[0, 0, 0], target.at[slot], here.line(here.near))
        for source, target in ((parts, landed), (dots_parts, dots_landed))
        for slot in range(3)
    ]
    lines = [
        wire.later(job.mine(), target.at[slots[i]], here.line(order[i]), base + 3 * k + slots[i])
        for k, (group, target) in enumerate(((jobs, landed), (dots_jobs, dots_landed)))
        for i, job in enumerate(group)
        if i
    ]
    planes[0].first()
    own.wait()
    own_few.wait()
    for copy in few_line:
        copy.wait_recv()
    few_plane.first()

    def where(step):
        group, half = step // 2, step % 2
        late = group // 2
        number = (here.depth + group) % 2 * (1 - late) + group * late
        return group, here.mirrored(number), (here.y + half) % 2

    def loads(step):
        _, z, y = where(step)
        at = pl.ds(4 * y, 4)
        return [
            pltpu.make_async_copy(x_out.at[z, at], x_buf, fetch.at[0]),
            pltpu.make_async_copy(g.at[z, at], g_buf, fetch.at[1]),
        ]

    def stores(step):
        _, z, y = where(step)
        at = pl.ds(4 * y, 4)
        return [
            pltpu.make_async_copy(o_buf, out_parts.at[pl.ds(2 * y, 2), :, z], store.at[0]),
            pltpu.make_async_copy(p_buf, pre_out.at[z, at], store.at[1]),
            pltpu.make_async_copy(h_buf, weighted_out.at[z, at], store.at[2]),
        ]

    def scatter(i, phase):
        for job in (jobs[i], dots_jobs[i]):
            getattr(job, phase)()
        if phase == "third" and i:
            lines[i - 1].start()
            lines[3 + i - 1].start()

    def arrived(step):
        for chip in (0, 1):
            planes[step // 2].twins[step % 2 * 2 + chip].wait_recv()

    def begin(i):
        return functools.partial(scatter, i, "begin")

    def first(i):
        return functools.partial(scatter, i, "first")

    def second(i):
        return functools.partial(scatter, i, "second")

    def third(i):
        return functools.partial(scatter, i, "third")

    before = [
        [few_plane.second, few_plane.third, few_plane.finish, planes[0].third, planes[1].second],
        [line.second, planes[2].first, planes[1].third],
        [line.third, planes[3].first, planes[2].second, begin(0)],
        [planes[2].third, planes[3].second, first(0)],
        [planes[3].third, second(0), begin(1)],
        [third(0), first(1)],
        [second(1), begin(2)],
        [third(1), first(2)],
    ]
    after = [begin(3), second(2), first(3), third(2), second(3), third(3)]

    planes[0].second()
    line.first()
    planes[1].first()
    arrived(0)
    for copy in loads(0):
        copy.start()
    for copy in weights:
        copy.wait()

    @pl.loop(0, STEPS)
    def _(step):
        for number in range(STEPS):

            @pl.when(step == number)
            def _():
                for action in before[number]:
                    action()
                if number + 1 < STEPS:
                    arrived(number + 1)

        group, z, y = where(step)
        for b in range(4):
            block = few_all[4 * y + b, z]
            block = jnp.concatenate([block, jnp.zeros((LANES - few_rows, LANES), F32)], axis=0)
            by_buf[pl.ds(b * rows, rows)] = block.T
        for copy in loads(step):
            copy.wait()
        pre_buf[...] = times_back(x_buf[...].reshape(chunk, width), w_both[...])
        back_buf[...] = times_back(g_buf[...].reshape(chunk, width), w_down[...])

        @pl.when(step + 1 < STEPS)
        def _():
            for copy in loads(step + 1):
                copy.start()

        @pl.when(step >= 1)
        def _():
            for copy in stores(step - 1):
                copy.wait()

        size = 32

        @pl.loop(0, chunk // size)
        def _(i):
            at = pl.ds(pl.multiple_of(i * size, size), size)
            gate_pre, up_pre = pre_buf[at, :units], pre_buf[at, units:]
            back = back_buf[at]
            lane = lax.broadcasted_iota(jnp.int32, (size, LANES), 1)
            factor = by_buf[at]
            by_route = jnp.sum(jnp.where(lane == here.c, factor, 0.0), axis=1, keepdims=True)
            by_switch = jnp.sum(jnp.where(lane == PLANE, factor, 0.0), axis=1, keepdims=True)
            is_routed = lax.broadcasted_iota(jnp.int32, (size, units), 1) < routed
            by = jnp.where(is_routed, by_route, by_switch)
            sigma = jax.nn.sigmoid(gate_pre)
            act = gate_pre * sigma
            hidden = act * up_pre
            product = hidden * back
            routed_dot = jnp.sum(jnp.where(is_routed, product, 0.0), axis=1, keepdims=True)
            shared_dot = jnp.sum(jnp.where(is_routed, 0.0, product), axis=1, keepdims=True)
            dot_buf[at] = jnp.where(
                lane == here.c, routed_dot, jnp.where(lane == PLANE, shared_dot, 0.0)
            )
            back = back * by
            block, inner = i // (rows // size), i % (rows // size)
            inside = pl.ds(pl.multiple_of(inner * size, size), size)
            h_buf[block, inside] = (hidden * by).astype(BF16)
            slope = sigma * (1.0 + gate_pre * (1.0 - sigma))
            p_buf[block, inside, :units] = (back * up_pre * slope).astype(BF16)
            p_buf[block, inside, units:] = (back * act).astype(BF16)

        for b in range(4):
            dots_parts[group, 2 * y + b // 2, b % 2] = dot_buf[pl.ds(b * rows, rows)].T[:few_rows]

        @pl.loop(0, width // TILE)
        def _(i):
            at = pl.ds(pl.multiple_of(i * TILE, TILE), TILE)
            both = p_buf[...].reshape(chunk, 2 * units)
            tile = dot(both, w_both[:, at]).astype(BF16)
            parts[group, pl.ds(2 * y, 2), :, :, at] = tile.reshape(2, 2, rows, TILE)
            weighted = h_buf[...].reshape(chunk, units)
            tile = dot(weighted, w_down[:, at]).astype(BF16)
            o_buf[:, :, :, at] = tile.reshape(2, 2, rows, TILE)

        for copy in stores(step):
            copy.start()

    for action in after:
        action()
    for copy in stores(STEPS - 1):
        copy.wait()
    for copy in arrivals:
        copy.wait_recv()
    size = 32

    @pl.loop(0, rows // size)
    def _(i):
        at = pl.ds(pl.multiple_of(i * size, size), size)
        value = jobs[0].mine()[at].astype(F32)
        for j in range(3):
            value += landed[j, at].astype(F32)
        sum_out[at] = value

    dots_out[...] = dots_jobs[0].mine()[...] + dots_landed[0] + dots_landed[1] + dots_landed[2]
    line.finish()
    wire.close()


def feed_forward(x, few, g, mixed, shared, routed_down, shared_down, units):
    rows, width = x.shape
    copies = 3 + LINE_GATHER_COPIES + 5 * PLANE_GATHER_COPIES + 8 * PLANE_SCATTER_COPIES + 12
    return call(
        ffn_kernel,
        2,
        [
            ((LINE, PLANE, rows, width), BF16),
            ((rows, width), F32),
            (few.shape, F32),
            ((4, 2, LINE, rows, width), BF16),
            ((LINE, PLANE, rows, 2 * units), BF16),
            ((LINE, PLANE, rows, units), BF16),
        ],
        [x, few, g.reshape(LINE, PLANE, rows, width), mixed, shared, routed_down, shared_down],
        wires(copies)
        + [
            pltpu.SemaphoreType.DMA((14,)),
            pltpu.SemaphoreType.DMA((2,)),
            pltpu.SemaphoreType.DMA((3,)),
            pltpu.VMEM((2 * units, width), BF16),
            pltpu.VMEM((units, width), BF16),
            pltpu.VMEM((PLANE, LINE) + few.shape, F32),
            pltpu.VMEM((4, 4, 2, rows, width), BF16),
            pltpu.VMEM((3, rows, width), BF16),
            pltpu.VMEM((4, 4, 2) + few.shape, F32),
            pltpu.VMEM((3,) + few.shape, F32),
            pltpu.VMEM((4, rows, width), BF16),
            pltpu.VMEM((4, rows, width), BF16),
            pltpu.VMEM((2, 2, rows, width), BF16),
            pltpu.VMEM((4, rows, 2 * units), BF16),
            pltpu.VMEM((4, rows, units), BF16),
            pltpu.VMEM((4 * rows, 2 * units), F32),
            pltpu.VMEM((4 * rows, units), F32),
            pltpu.VMEM((4 * rows, LANES), F32),
            pltpu.VMEM((4 * rows, LANES), F32),
        ]
        + scatter_room(rows, width, BF16) * 4
        + scatter_room(few.shape[0], LANES, F32) * 4,
        out_specs=[HBM, VMEM, VMEM, HBM, HBM, HBM],
        in_specs=[VMEM, VMEM] + [HBM] * 5,
    )


def fan_kernel(block, after, out, send, recv, local):
    here, wire = Place(), Wire(send, recv)
    greet([here.plane(c) for c in (here.twin, here.across, here.along)])
    half = block.shape[0] // 2
    mine = pltpu.make_async_copy(block, out.at[here.c], local.at[0])
    mine.start()
    jobs = []
    for i in range(2):
        at = pl.ds(i * half, half)
        jobs.append(
            PlaneGather(
                wire, here, functools.partial(lambda at, c: out.at[c, at], at), block.at[at]
            ).first()
        )
    for job in jobs:
        job.second()
    for job in jobs:
        job.third()
    for job in jobs:
        job.finish()
    mine.wait()
    wire.close()


def fan_plane(block, after):
    return call(
        fan_kernel,
        5,
        [((PLANE,) + block.shape, block.dtype)],
        [block, after],
        wires(2 * PLANE_GATHER_COPIES) + [pltpu.SemaphoreType.DMA((1,))],
        in_specs=[VMEM, HBM],
    )[0].reshape(PLANE * block.shape[0], block.shape[1])


def end_kernel(
    parts, three, output, shared, bias, terms,
    out, three_out, output_out, shared_mid, shared_out, bias_out, terms_out,
    send, recv, local, held, three_held, output_held, *rooms
):
    here, wire = Place(), Wire(send, recv)
    room, three_room, output_room = rooms[:5], rooms[5:7], rooms[7:9]
    terms_in, terms_own, terms_line = rooms[9:]
    others = [(here.c + step) % PLANE for step in range(1, PLANE)]
    greet([here.plane(c) for c in others] + [here.line(z) for z in here.on_line()])
    on_line = here.on_line()
    loads = [
        pltpu.make_async_copy(three.at[:, z], three_held.at[z], local.at[z]) for z in range(LINE)
    ]
    loads += [
        pltpu.make_async_copy(parts, held, local.at[4]),
        pltpu.make_async_copy(output, output_held, local.at[5]),
        pltpu.make_async_copy(terms.at[here.c], terms_own, local.at[6]),
        pltpu.make_async_copy(bias, bias_out.at[here.z], local.at[7]),
    ]
    shared_own = pltpu.make_async_copy(shared.at[:, here.z], shared_mid.at[here.z], local.at[8])
    for copy in loads + [shared_own]:
        copy.start()
    job = PlaneScatter(wire, here, held, room)
    three_line = LineScatter(
        wire, here, [three_held.at[here.mirrored(i)] for i in range(4)], three_room
    )
    output_line = LineScatter(
        wire, here, [output_held.at[here.mirrored(i)] for i in range(4)], output_room
    )
    for copy in loads[:4]:
        copy.wait()
    three_line.begin()
    loads[4].wait()
    job.begin()
    shared_line = [
        wire.push(shared.at[:, z], shared_mid.at[here.z], here.line(z)) for z in on_line
    ]
    for copy in loads[5:]:
        copy.wait()
    output_line.begin()
    terms_plane = [
        wire.push(terms.at[c], terms_in.at[j], here.plane(c)) for j, c in enumerate(others)
    ]
    bias_line = [wire.push(bias, bias_out.at[here.z], here.line(z)) for z in on_line]
    job.first()
    job.second()
    job.third()
    out[...] = job.mine()[...].astype(F32)
    for copy in terms_plane:
        copy.wait_recv()
    total = terms_own[...]
    for j in range(PLANE - 1):
        total += terms_in[j]
    terms_own[...] = total
    terms_last = [
        wire.push(terms_own.at[z], terms_line.at[j], here.line(z)) for j, z in enumerate(on_line)
    ]
    three_line.first()
    output_line.first()
    three_line.second()
    shared_own.wait()
    for copy in shared_line:
        copy.wait_recv()
    shared_kept = pltpu.make_async_copy(shared_mid.at[:, here.c], shared_out.at[here.c], local.at[8])
    shared_kept.start()
    shared_plane = [
        wire.push(shared_mid.at[:, c], shared_out.at[here.c], here.plane(c)) for c in others
    ]
    output_line.second()
    three_line.third()
    three_plane = [
        wire.push(three_held.at[here.z, c], three_out.at[here.c], here.plane(c)) for c in others
    ]
    kept = pltpu.make_async_copy(three_held.at[here.z, here.c], three_out.at[here.c], local.at[0])
    kept.start()
    output_line.third()
    output_out[...] = output_held[here.z].astype(F32)
    for copy in terms_last:
        copy.wait_recv()
    terms_out[...] = terms_own[here.z] + terms_line[0] + terms_line[1] + terms_line[2]
    for copy in bias_line + shared_plane + three_plane:
        copy.wait_recv()
    kept.wait()
    shared_kept.wait()
    wire.close()


def line_room(shape, kind):
    return [pltpu.VMEM((3,) + shape, kind), pltpu.VMEM((2,) + shape, kind)]


def end_transfers(parts, three, output, shared, bias, terms):
    rows, width = parts.shape[0] // PLANE, parts.shape[1]
    _, _, owned, wide = three.shape
    copies = PLANE_SCATTER_COPIES + 2 * LINE_SCATTER_COPIES + 3 + 7 + 3 + 3 + 7 + 7
    out = call(
        end_kernel,
        6,
        [
            ((rows, width), F32),
            ((PLANE, owned, wide), BF16),
            ((owned, width), F32),
            ((LINE, PLANE) + shared.shape[2:], BF16),
            ((PLANE, LINE) + shared.shape[2:], BF16),
            ((LINE,) + bias.shape, F32),
            (terms.shape[2:], F32),
        ],
        [parts.reshape(4, 2, rows, width), three, output, shared, bias, terms],
        wires(copies)
        + [
            pltpu.SemaphoreType.DMA((9,)),
            pltpu.VMEM((4, 2, rows, width), BF16),
            pltpu.VMEM((LINE, PLANE, owned, wide), BF16),
            pltpu.VMEM((LINE, owned, width), BF16),
        ]
        + scatter_room(rows, width, BF16)
        + line_room((PLANE, owned, wide), BF16)
        + line_room((owned, width), BF16)
        + [
            pltpu.VMEM((PLANE - 1,) + terms.shape[1:], F32),
            pltpu.VMEM(terms.shape[1:], F32),
            pltpu.VMEM((3,) + terms.shape[2:], F32),
        ],
        out_specs=[VMEM, HBM, VMEM, HBM, HBM, HBM, VMEM],
        in_specs=[HBM] * 4 + [VMEM, HBM],
    )
    return out[:3] + out[4:]


def rms_scale(values):
    return lax.rsqrt(jnp.mean(values * values, axis=-1, keepdims=True) + EPS)


def rope_tables(places, head_size):
    half = head_size // 2
    freqs = jnp.exp(jnp.arange(half, dtype=F32) * (-2.0 * math.log(ROPE_BASE) / head_size))
    angles = places.astype(F32)[:, None] * freqs[None, :]
    return (jnp.cos(angles)[:, None, :], jnp.sin(angles)[:, None, :])


def rotate(values, cosine, sine):
    half = values.shape[-1] // 2
    first = values[..., :half]
    second = values[..., half:]
    return jnp.concatenate(
        [first * cosine - second * sine, second * cosine + first * sine], axis=-1
    )


def dot(left, right):
    return jnp.dot(left, right, preferred_element_type=F32)


def times_back(left, right):
    return lax.dot_general(left, right, (((1,), (1,)), ((), ())), preferred_element_type=F32)


def outer_sum(left, right):
    return lax.dot_general(left, right, (((0,), (0,)), ((), ())), preferred_element_type=F32)


def gather_plane(shard):
    return lax.all_gather(shard, "ctx", axis=0, tiled=True)


def scatter_plane(partial):
    return lax.psum_scatter(partial, "ctx", scatter_dimension=0, tiled=True)


def scatter_line(partial):
    return lax.psum_scatter(partial, "fsdp", scatter_dimension=0, tiled=False)


def over(step, carry, items, unrolled):
    if not unrolled:
        return lax.scan(step, carry, items)
    outs = []
    for i in range(jax.tree.leaves(items)[0].shape[0]):
        carry, out = step(carry, jax.tree.map(lambda item: item[i], items))
        outs.append(out)
    return carry, jax.tree.map(lambda *parts: jnp.stack(parts), *outs)


def blocks(length):
    return length // min(length, BLOCK)


def cut(array, axis=0):
    shape = array.shape
    count = blocks(shape[axis])
    shape = shape[:axis] + (count, shape[axis] // count) + shape[axis + 1 :]
    return jnp.moveaxis(array.reshape(shape), axis, 0)


def attend(queries, keys, values, starts):
    length = queries.shape[0]
    scale = 1.0 / math.sqrt(HEAD)
    cols = jnp.arange(length, dtype=jnp.int32)[None, :]

    def step(carry, items):
        part, low, rows = items
        mask = ((cols <= rows[:, None]) & (cols >= low[:, None]))[None]
        scores = jnp.einsum("qhd,khd->hqk", part, keys, preferred_element_type=F32)
        scores = jnp.where(mask, scores * scale, MASKED)
        best = jnp.max(scores, axis=-1, keepdims=True)
        weights = jnp.exp(scores - best)
        total = jnp.sum(weights, axis=-1, keepdims=True)
        probs = (weights / total).astype(BF16)
        out = jnp.einsum("hqk,khd->qhd", probs, values, preferred_element_type=F32)
        return carry, (out, best + jnp.log(total))

    items = (cut(queries), cut(starts), cut(cols[0]))
    _, (outs, logs) = over(step, 0, items, blocks(length) == 1)
    return outs.reshape(queries.shape), jnp.moveaxis(logs, 0, 1).reshape(-1, length, 1)


def attend_back(queries, keys, values, starts, logs, grad_attn, delta):
    length = queries.shape[0]
    scale = 1.0 / math.sqrt(HEAD)
    cols = jnp.arange(length, dtype=jnp.int32)[None, :]

    def step(carry, items):
        grad_keys, grad_values = carry
        part, low, rows, log, grad, less = items
        mask = ((cols <= rows[:, None]) & (cols >= low[:, None]))[None]
        scores = jnp.einsum("qhd,khd->hqk", part, keys, preferred_element_type=F32)
        probs = jnp.where(mask, jnp.exp(scores * scale - log), 0.0)
        grad_probs = jnp.einsum("qhd,khd->hqk", grad, values, preferred_element_type=F32)
        grad_scores = (probs * (grad_probs - less[:, :, None])).astype(BF16)
        grad_queries = scale * jnp.einsum(
            "hqk,khd->qhd", grad_scores, keys, preferred_element_type=F32
        )
        grad_keys += scale * jnp.einsum(
            "hqk,qhd->khd", grad_scores, part, preferred_element_type=F32
        )
        grad_values += jnp.einsum(
            "hqk,qhd->khd", probs.astype(BF16), grad, preferred_element_type=F32
        )
        return (grad_keys, grad_values), grad_queries

    zeros = jnp.zeros(keys.shape, F32)
    items = (cut(queries), cut(starts), cut(cols[0]), cut(logs, 1), cut(grad_attn), cut(delta, 1))
    carry, grad_queries = over(step, (zeros, zeros), items, blocks(length) == 1)
    return grad_queries.reshape(queries.shape), carry[0], carry[1]


def body(
    tokens,
    positions,
    routes,
    cotangent,
    attn_gain,
    query_weight,
    key_weight,
    value_weight,
    query_bias,
    key_bias,
    value_bias,
    output_weight,
    ffn_gain,
    router_weight,
    expert_gate,
    expert_up,
    expert_down,
    shared_gate,
    shared_up,
    shared_down,
    shared_sigmoid,
):
    plane, line = lax.axis_size("ctx"), lax.axis_size("fsdp")
    place = lax.axis_index("ctx")
    rows, width = tokens.shape[1], tokens.shape[2]
    length = plane * rows
    experts = router_weight.shape[1]
    groups = math.gcd(HEADS, plane)
    share = plane // groups
    heads = HEADS // groups
    span = heads * HEAD
    owned = width // (plane * line)
    group = place // share

    fast = (plane, line) == (PLANE, LINE) and share == 1
    three = jnp.stack([query_weight, key_weight, value_weight])
    routed_units, shared_units = expert_down.shape[1], shared_down.shape[0]
    columns = [attn_gain, query_bias, key_bias, value_bias, ffn_gain, shared_sigmoid]
    columns = jnp.concatenate([jnp.stack(columns, axis=1), router_weight], axis=1)
    x_own, g_own = tokens[0], cotangent[0]
    shared = [w.reshape(owned, plane * line, shared_units) for w in (shared_gate, shared_up)]
    shared = jnp.concatenate(shared, axis=2).transpose(1, 0, 2)
    routed = jnp.stack([expert_gate[0].T, expert_up[0].T]).reshape(2, line, routed_units, -1)
    routed = routed.transpose(1, 0, 2, 3)
    if fast:
        high, low = positions[0] // 64, positions[0] % 64
        digits = jnp.stack([high, low]).reshape(2 * (rows // owned), owned).T.astype(BF16)
        small = jnp.concatenate([columns, digits], axis=1)
        marks = small.shape[1]
        small = jnp.pad(small, ((0, 0), (0, LANES - marks)))
        sent = three.reshape(3, owned, plane, span).transpose(2, 1, 0, 3)
        g_all = lax.all_gather(g_own, ("fsdp", "ctx"), axis=0, tiled=True)
        x_all, w_three, w_output, small, shared = start_transfers(
            x_own,
            sent.reshape(plane, owned, 3 * span),
            output_weight,
            small,
            shared.reshape(plane, line, owned, 2 * shared_units),
        )
        routed = routed.reshape(line, 2 * routed_units, -1)
        routed = lax.all_to_all(routed, "fsdp", split_axis=0, concat_axis=0, tiled=True)
        x_all = x_all.reshape(length, width)
        w_three = w_three.reshape(width, 3 * span)
        w_output = w_output.reshape(span, width)
        digits = lax.dynamic_index_in_dim(small, lax.axis_index("fsdp"), 1, keepdims=False)
        digits = digits[:, :, columns.shape[1] : marks].astype(jnp.int32)
        digits = digits.transpose(0, 2, 1).reshape(plane, 2, rows)
        places = (digits[:, 0] * 64 + digits[:, 1]).reshape(length)
        small = small.reshape(width, LANES)[:, : columns.shape[1]]
    else:
        small = lax.all_gather(columns, BOTH, axis=0, tiled=True)
        places = lax.all_gather(positions[0], "ctx", axis=0, tiled=True)
        x_all = gather_plane(x_own)
        whole = lax.all_gather(three, BOTH, axis=1, tiled=True)
        whole = lax.dynamic_slice_in_dim(whole, group * span, span, 2)
        w_three = whole.transpose(1, 0, 2).reshape(width, 3 * span)
        w_output = lax.all_gather(output_weight, BOTH, axis=0, tiled=True)
        w_output = lax.dynamic_slice_in_dim(w_output, group * span, span, 0)
    gain_in = small[:, 0].astype(F32)
    gain_mid = small[:, 4].astype(F32)
    w_switch = small[:, 5]
    w_router = small[:, 6:]
    biases = lax.dynamic_slice_in_dim(small[:, 1:4], group * span, span, 0).astype(F32)
    biases = biases.T.reshape(3 * span)
    used = routed_units + shared_units
    units = -(-used // LANES) * LANES

    states = x_all.astype(F32)
    starts = jnp.arange(length, dtype=jnp.int32) - places
    unit_in = states * rms_scale(states)
    normed = (unit_in * gain_in[None, :]).astype(BF16)
    cosine, sine = rope_tables(places, HEAD)
    pre = (dot(normed, w_three) + biases[None, :]).reshape(length, 3, heads, HEAD)
    queries = rotate(pre[:, 0], cosine, sine).astype(BF16)
    keys = rotate(pre[:, 1], cosine, sine).astype(BF16)
    values = pre[:, 2].astype(BF16)
    attn_rows, logs = attend(queries, keys, values, starts)
    if share > 1:
        mine = jnp.arange(length, dtype=jnp.int32) // (length // share) == place % share
        attn_rows = jnp.where(mine[:, None, None], attn_rows, 0.0)
    attn_low = attn_rows.reshape(length, span).astype(BF16)
    branch = dot(attn_low, w_output).astype(BF16)
    if fast:
        branch, shared = fold_plane(branch, shared)
    else:
        branch = scatter_plane(branch).astype(F32)
    mid = x_own.astype(F32) + branch

    scale_mid = rms_scale(mid)
    unit_mid = mid * scale_mid
    normed2 = (unit_mid * gain_mid[None, :]).astype(BF16)
    router_probs = jax.nn.softmax(dot(normed2, w_router), axis=-1)
    picks = routes[0][:, :, None] == jnp.arange(experts, dtype=jnp.int32)[None, None, :]
    hits = jnp.any(picks, axis=1)
    switch = jax.nn.sigmoid(dot(normed2, w_switch[:, None]))
    factors = jnp.concatenate([jnp.where(hits, router_probs, 0.0), switch], axis=1)
    mine = jnp.arange(experts, dtype=jnp.int32) == place

    def hidden_units(x_all, g_all, by_route, by_switch, w_both, w_down):
        number = jnp.arange(units, dtype=jnp.int32)
        by = jnp.where(number < routed_units, by_route[:, None], by_switch[:, None])
        pre = times_back(x_all, w_both)
        gate_pre, up_pre = pre[:, :units], pre[:, units:]
        grad_hidden = times_back(g_all, w_down)
        sigma = jax.nn.sigmoid(gate_pre)
        act = gate_pre * sigma
        hidden = act * up_pre
        product = hidden * grad_hidden
        routed_dot = jnp.sum(product[:, :routed_units], axis=1)
        shared_dot = jnp.sum(product[:, routed_units:used], axis=1)
        weighted = (hidden * by).astype(BF16)
        slope = sigma * (1.0 + gate_pre * (1.0 - sigma))
        grad_hidden = grad_hidden * by
        grad_pre = jnp.concatenate([grad_hidden * up_pre * slope, grad_hidden * act], axis=1)
        grad_pre = grad_pre.astype(BF16)
        grad_part = dot(grad_pre, w_both).astype(BF16)
        out_part = dot(weighted, w_down).astype(BF16)
        terms = (outer_sum(grad_pre, x_all), outer_sum(weighted, g_all))
        return terms, out_part, grad_part, routed_dot, shared_dot

    def units_of(routed, shared, spare):
        return jnp.concatenate([routed[0], shared[0], spare, routed[1], shared[1], spare], axis=0)

    def parts_of(term):
        routed = [term[:routed_units], term[units : units + routed_units]]
        shared = [term[routed_units:used], term[units + routed_units : units + used]]
        return jnp.stack(routed), jnp.stack(shared)

    if fast:
        few = jnp.pad(factors.T, ((0, 16 - experts - 1), (0, 0)))
        shared = shared.reshape(width, 2 * shared_units).T
        x_all, grad_ffn, dots, out_part, grad_pre, weighted = feed_forward(
            normed2, few, g_all, routed, shared, expert_down[0], shared_down, units
        )
        ffn = scatter_plane(out_part.reshape(plane * line * rows, width))
        ffn = scatter_line(ffn.reshape(line, rows, width)).astype(F32)
        term_both = outer_sum(
            grad_pre.reshape(line * length, 2 * units), x_all.reshape(line * length, width)
        )
        term_down = outer_sum(weighted.reshape(line * length, units), g_all)
        routed, shared = parts_of(term_both.astype(BF16))
        routed = routed.reshape(2 * routed_units, line, -1).transpose(1, 0, 2)
        routed_sent = routed
        routed = lax.all_to_all(routed, "fsdp", split_axis=0, concat_axis=0, tiled=True)
        routed = routed.reshape(line, 2, routed_units, -1)
        shared = shared.reshape(2 * shared_units, width).T
        shared = shared.reshape(plane, line, owned, 2 * shared_units)
        dots = dots[: experts + 1].T
    else:
        routed = lax.all_to_all(routed, "fsdp", split_axis=0, concat_axis=0, tiled=True)
        routed = routed.transpose(1, 2, 0, 3).reshape(2, routed_units, width)
        spare = jnp.zeros((units - used, width), BF16)
        w_down = jnp.concatenate([expert_down[0], shared_down, spare], axis=0)
        factors = lax.all_gather(factors, ("fsdp", "ctx"), axis=0, tiled=True)
        factors = factors.reshape(line, length, experts + 1)
        x_line = lax.all_gather(normed2, "fsdp", axis=0, tiled=False)
        g_line = lax.all_gather(g_own, "fsdp", axis=0, tiled=False)

        shared = lax.all_to_all(shared, BOTH, split_axis=0, concat_axis=0, tiled=True)
        shared = shared.reshape(width, 2, shared_units).transpose(1, 2, 0)
        w_both = units_of(routed, shared, spare)

        def step(terms, items):
            x_part, g_part, factor = items
            by_route = jnp.sum(jnp.where(mine, factor[:, :experts], 0.0), axis=1)
            more, out_part, grad_part, routed_dot, shared_dot = hidden_units(
                gather_plane(x_part), gather_plane(g_part), by_route, factor[:, experts], w_both, w_down
            )
            dots = jnp.where(mine, routed_dot[:, None], 0.0)
            dots = jnp.concatenate([dots, shared_dot[:, None]], axis=1)
            terms = tuple(term + part for term, part in zip(terms, more))
            return terms, (scatter_plane(out_part), scatter_plane(grad_part), dots)

        terms = tuple(jnp.zeros(w.shape, F32) for w in (w_both, w_down))
        terms, (out_parts, grad_parts, dots) = lax.scan(step, terms, (x_line, g_line, factors))
        term_both, term_down = terms
        grad_ffn = scatter_line(grad_parts).astype(F32)
        ffn = scatter_line(out_parts).astype(F32)
        dots = dots.reshape(line, plane, rows, experts + 1)
        dots = lax.psum_scatter(dots, "ctx", scatter_dimension=1, tiled=False)
        dots = scatter_line(dots)

        routed, shared = parts_of(term_both.astype(BF16))
        grad_shared_gate, grad_shared_up = [
            lax.all_to_all(t.T, BOTH, split_axis=0, concat_axis=1, tiled=True).astype(F32)
            for t in shared
        ]
        routed = routed.reshape(2, routed_units, line, -1).transpose(2, 0, 1, 3)
        routed = lax.all_to_all(routed, "fsdp", split_axis=0, concat_axis=0, tiled=True)
    grad_expert_down = term_down[:routed_units][None]
    grad_shared_down = term_down[routed_units:used]

    grad_out = cotangent[0].astype(F32)
    grad_probs = jnp.where(hits, dots[:, :experts], 0.0)
    grad_logits = (
        router_probs * (grad_probs - jnp.sum(router_probs * grad_probs, axis=-1, keepdims=True))
    ).astype(BF16)
    grad_switch = dots[:, experts:] * switch * (1.0 - switch)
    grad_normed2 = (
        grad_ffn + times_back(grad_logits, w_router) + grad_switch * w_switch.astype(F32)[None, :]
    )
    scaled_mid = grad_normed2 * gain_mid[None, :]
    grad_mid = grad_out + scale_mid * (
        scaled_mid - unit_mid * jnp.mean(scaled_mid * unit_mid, axis=-1, keepdims=True)
    )
    terms = jnp.concatenate(
        [
            jnp.sum(grad_normed2 * unit_mid, axis=0)[:, None],
            jnp.sum(grad_switch * normed2.astype(F32), axis=0)[:, None],
            outer_sum(normed2, grad_logits),
        ],
        axis=1,
    )

    grad_branch = grad_mid.astype(BF16)
    if fast:
        grad_branch = fan_plane(grad_branch, routed_sent)
    else:
        grad_branch = gather_plane(grad_branch)
    routed = routed.transpose(1, 3, 0, 2).reshape(2, 1, -1, line * routed_units).astype(F32)
    grad_attn = times_back(grad_branch, w_output).reshape(length, heads, HEAD).astype(BF16)
    if share > 1:
        mine = jnp.arange(length, dtype=jnp.int32) // (length // share) == place % share
        grad_attn = jnp.where(mine[:, None, None], grad_attn, 0)
    delta = jnp.sum(grad_attn.astype(F32) * attn_rows, axis=-1).T
    grad_queries, grad_keys, grad_values = attend_back(
        queries, keys, values, starts, logs, grad_attn, delta
    )
    grad_pre = jnp.concatenate(
        [
            rotate(grad_queries, cosine, -sine).reshape(length, span),
            rotate(grad_keys, cosine, -sine).reshape(length, span),
            grad_values.reshape(length, span),
        ],
        axis=1,
    ).astype(BF16)
    grad_part = times_back(grad_pre, w_three).astype(BF16)
    term_three = outer_sum(normed, grad_pre)
    term_output = outer_sum(attn_low, grad_branch)
    term_bias = jnp.sum(grad_pre.astype(F32), axis=0)
    if fast:
        count = terms.shape[1]
        terms = terms.reshape(plane, line, owned * count)
        terms = jnp.pad(terms, ((0, 0), (0, 0), (0, 8 * LANES - owned * count)))
        grad_normed, grad_three, grad_output, shared, term_bias, terms = end_transfers(
            grad_part,
            term_three.astype(BF16).reshape(plane, line, owned, 3 * span),
            term_output.astype(BF16).reshape(line, owned, width),
            shared,
            jnp.broadcast_to(term_bias[None], (8, 3 * span)),
            terms.reshape(plane, line, 8, LANES),
        )
        grad_three = grad_three.reshape(plane, owned, 3, span).transpose(2, 1, 0, 3)
        grad_three = grad_three.reshape(3, owned, width).astype(F32)
        term_bias = jnp.sum(term_bias[:, 0], axis=0).reshape(3, line, owned)
        grad_bias = lax.dynamic_index_in_dim(term_bias, lax.axis_index("fsdp"), 1, keepdims=False)
        terms = terms.reshape(-1)[: owned * count].reshape(owned, count)
        shared = shared.reshape(plane * line, owned, 2 * shared_units)
        grad_shared_gate, grad_shared_up = [
            part.transpose(1, 0, 2).reshape(owned, -1).astype(F32)
            for part in (shared[:, :, :shared_units], shared[:, :, shared_units:])
        ]
    else:
        grad_normed = scatter_plane(grad_part).astype(F32)
        zeros = jnp.zeros((3, width, width), BF16)
        spread = lax.dynamic_update_slice_in_dim(
            zeros, term_three.astype(BF16).reshape(width, 3, span).transpose(1, 0, 2), group * span, 2
        )
        grad_three = lax.psum_scatter(spread, BOTH, scatter_dimension=1, tiled=True).astype(F32)
        spread = lax.dynamic_update_slice_in_dim(
            zeros[0], term_output.astype(BF16), group * span, 0
        )
        grad_output = lax.psum_scatter(spread, BOTH, scatter_dimension=0, tiled=True).astype(F32)
        spread = lax.dynamic_update_slice_in_dim(
            jnp.zeros((3, width), F32), term_bias.reshape(3, span), group * span, 1
        )
        grad_bias = lax.psum_scatter(spread, BOTH, scatter_dimension=1, tiled=True)
        terms = lax.psum_scatter(terms, BOTH, scatter_dimension=0, tiled=True)
    grad_attn_gain = jnp.sum(three.astype(F32) * grad_three, axis=(0, 2)) / attn_gain.astype(F32)
    own_states = tokens[0].astype(F32)
    scale_in = rms_scale(own_states)
    own_unit = own_states * scale_in
    scaled_in = grad_normed * gain_in[None, :]
    grad_states = grad_mid + scale_in * (
        scaled_in - own_unit * jnp.mean(scaled_in * own_unit, axis=-1, keepdims=True)
    )
    return (
        (mid + ffn).astype(BF16)[None],
        grad_states[None],
        grad_attn_gain,
        grad_three[0],
        grad_three[1],
        grad_three[2],
        grad_bias[0],
        grad_bias[1],
        grad_bias[2],
        grad_output,
        terms[:, 0],
        terms[:, 2:],
        routed[0],
        routed[1],
        grad_expert_down,
        grad_shared_gate,
        grad_shared_up,
        grad_shared_down,
        terms[:, 1],
    )


def solution(mesh):
    tokens, flat, both, routed = (
        P("fsdp", "ctx", None),
        P(BOTH),
        P(BOTH, None),
        P("ctx", "fsdp", None),
    )
    weights = (flat, both, both, both, flat, flat, flat, both, flat, both)
    weights += (routed, routed, routed, both, both, both, flat)
    return jax.shard_map(
        body,
        mesh=mesh,
        in_specs=(tokens, P("fsdp", "ctx"), tokens, tokens) + weights,
        out_specs=(tokens, tokens) + weights,
        check_vma=False,
    )
```
